512 devices in a mesh: section: 16 (over x, y_lo, core), dp: 32 (over y_hi, z).
Axes of the slice: x: 4, y: 8 (y_hi: 4, y_lo: 2; y = y_hi * 2 + y_lo), z: 8, core: 2. Of those that a mesh axis runs over, the one named last changes fastest.
Arguments:
- hidden: bfloat16 [196608, 5120], P(('section', 'dp')), may hold values from -6 to 6
- targets: int32 [196608], P(('section', 'dp')), may hold values from 0 to 191
- head_weight: bfloat16 [5120, 192], P('section'), may hold values from -0.25155765 to 0.25155765
- norm_gain: float32 [5120], replicated, may hold values from 0.5 to 1.5
Outputs:
- weight_grad: float32 [5120, 192], P(('section', 'dp'))
- gain_grad: float32 [5120], replicated
The draws below stay inside these ranges and needn't reach their ends.
All inputs are finite; a program needn't handle non-finite values.
Results may differ from the reference program's by a relative error of at most 0.0029.
Values may be sent and summed in bfloat16 or wider, within the bound.
A program may use at most 64 MiB of HBM per device.

```python
import jax
import jax.numpy as jnp
from jax import lax

D = 5120
V = 192
TOK_DEV = 384
TOKENS = 196608


def shared_columns(key):
    return jnp.clip(jax.random.normal(key, (D, V), jnp.float32), -6.0, 6.0)


def draw_head_weight(key, part):
    limit = 18.0 * D ** (-0.5)
    base = shared_columns(key) * (3.0 * D ** (-0.5))
    return jnp.clip(base, -limit, limit).astype(jnp.bfloat16)


def draw_hidden(key, part):
    key = jax.random.fold_in(key, 12)
    rows = jnp.clip(jax.random.normal(key, (TOKENS, D), jnp.float32), -6.0, 6.0)
    return rows.astype(jnp.bfloat16)


def place_ends(array, rng, least, high):
    shape = array.shape
    index_at = [jax.random.randint(jax.random.fold_in(rng, axis), (), 0, shape[axis]) for axis in range(len(shape))]
    array = array.at[tuple(index_at)].set(least)
    longest = shape.index(max(shape))
    index_at[longest] = (index_at[longest] + 1) % shape[longest]
    return array.at[tuple(index_at)].set(high)


def setup_inputs(seed: int = 0) -> dict:
    key_list = jax.random.split(jax.random.key(seed), 5)
    return {
        "hidden": draw_hidden(jax.random.fold_in(key_list[4], 71), 0),
        "targets": place_ends(jax.random.randint(key_list[1], (TOKENS,), 0, V), jax.random.fold_in(key_list[1], 1), 0, V - 1).astype(jnp.int32),
        "head_weight": draw_head_weight(jax.random.fold_in(key_list[4], 71), 0),
        "norm_gain": jnp.clip(1.0 + 0.1 * jax.random.normal(key_list[3], (D,), jnp.float32), 0.5, 1.5),
    }


def block_terms(rows, goals, head_weight, norm_gain):
    values = rows.astype(jnp.float32)
    meansq = lax.optimization_barrier(jnp.mean(values * values, axis=-1, keepdims=True))
    normed = values * lax.rsqrt(meansq + 1e-05)
    scaled = (normed * norm_gain[None, :]).astype(jnp.bfloat16)
    logits = jnp.dot(scaled, head_weight, preferred_element_type=jnp.float32)
    probs = jax.nn.softmax(logits, axis=-1)
    onehot = (goals[:, None] == jnp.arange(logits.shape[1], dtype=jnp.int32)[None, :]).astype(jnp.float32)
    dlogits = ((probs - onehot) * (1.0 / TOK_DEV ** 0.5)).astype(jnp.bfloat16)
    wterm = jnp.einsum('td,tv->dv', scaled.astype(jnp.float32), dlogits.astype(jnp.float32))
    dscaled = jnp.einsum('tv,dv->td', dlogits.astype(jnp.float32), head_weight.astype(jnp.float32))
    gterm = lax.optimization_barrier(jnp.sum(dscaled * normed, axis=0))
    return (wterm, gterm)

def reference(hidden, targets, head_weight, norm_gain):
    blocks = TOKENS // TOK_DEV
    rows_all = hidden.reshape(blocks, TOK_DEV, D)
    goals_all = targets.reshape(blocks, TOK_DEV)

    def step(carry, item):
        wterm, gterm = block_terms(item[0], item[1], head_weight, norm_gain)
        return ((carry[0] + wterm, carry[1] + gterm), None)
    start = (jnp.zeros((D, V), jnp.float32), jnp.zeros((D,), jnp.float32))
    (weight_grad, gain_grad), unused = lax.scan(step, start, (rows_all, goals_all))
    return (weight_grad, gain_grad)
```

```python
import jax
import jax.numpy as jnp
from jax import lax
from jax.experimental import pallas as pl
from jax.experimental.pallas import tpu as pltpu
from jax.sharding import PartitionSpec as P

D = 5120
V = 192
TOK = 384
NX, NY, NZ = 4, 8, 8
QW = 640
MESH = pl.DeviceIdType.MESH
F32 = jnp.float32
BF16 = jnp.bfloat16
SCALE = 1.0 / TOK**0.5


def kernel(
    hid, tgt, w, gain, wg_out, gg_out,
    h, s, rv, wp, wu, logit, dlz, dle,
    a_keep, a_send, a_core, b_keep, b_send, b_core,
    ax_send, ax_recv, a_acc, ay_send, ay_recv, a_fin, az_send, az_recv,
    by_send, by_acc, by_recv, bx_send, bx_recv, b_fin, bz_send, bz_recv,
    g_loc, g_core, g_x, g_y, g_z, g_mine, g_full,
    hsem,
    wx_s, wx_r, wy_s, wy_r, wc_s, wc_r,
    ac_s, ac_r, bc_s, bc_r,
    ax_s, ax_r, ay_s, ay_r, az_s, az_r,
    by_s, by_r, bx_s, bx_r, bz_s, bz_r,
    gc_s, gc_r, gx_s, gx_r, gy_s, gy_r, gz_s, gz_r, gf_s, gf_r,
):
    sec = lax.axis_index("section")
    dp = lax.axis_index("dp")
    c = lax.rem(sec, 2)
    yl = lax.rem(lax.div(sec, 2), 2)
    x = lax.div(sec, 4)
    yh = lax.div(dp, NZ)
    z = lax.rem(dp, NZ)
    y = yh * 2 + yl
    oc = 1 - c

    def dev(x_, y_, z_, c_):
        return (x_ * 4 + lax.rem(y_, 2) * 2 + c_, lax.div(y_, 2) * NZ + z_)

    def xo(k):
        return lax.rem(x + k, NX)

    def yo(k):
        return lax.rem(y + k, NY)

    def zo(k):
        return lax.rem(z + k, NZ)

    def rcopy(src, dst, ss, rs, to):
        return pltpu.make_async_remote_copy(
            src_ref=src, dst_ref=dst, send_sem=ss, recv_sem=rs,
            device_id=to, device_id_type=MESH)

    hcopies = [
        pltpu.make_async_copy(hid.at[pl.ds(96 * i, 96)], h.at[pl.ds(96 * i, 96)], hsem.at[i])
        for i in range(4)
    ]
    for cp in hcopies:
        cp.start()

    barrier = pltpu.get_barrier_semaphore()
    peers = [dev(xo(k), y, z, c) for k in range(1, NX)]
    peers += [dev(x, yo(k), z, c) for k in range(1, NY)]
    peers += [dev(x, y, zo(k), c) for k in range(1, NZ)]
    peers += [dev(x, y, zo(k), oc) for k in range(NZ)]
    for p in peers:
        pl.semaphore_signal(barrier, inc=1, device_id=p, device_id_type=MESH)

    wp[sec, 0:320, :] = w[:, 0:128]
    wp[sec, 320:480, :] = jnp.concatenate([w[0:160, 128:192], w[160:320, 128:192]], axis=1)

    t_row = tgt[...].astype(F32)
    t_col = jnp.transpose(jnp.broadcast_to(t_row.reshape(1, TOK), (128, TOK)))

    pl.semaphore_wait(barrier, len(peers))

    started = []

    def go(cp):
        cp.start()
        started.append(cp)
        return cp

    wx = [None] * NX
    for k in (1, 3, 2):
        wx[k] = go(rcopy(wp.at[sec], wp.at[sec], wx_s.at[k], wx_r.at[k], dev(xo(k), y, z, c)))

    def shard(k, l, cc):
        return xo(NX - k if k else 0) * 4 + l * 2 + cc

    def fwd_y(k):
        sh = shard(k, yl, c)
        lo = go(rcopy(wp.at[sh, pl.ds(0, 240)], wp.at[sh, pl.ds(0, 240)],
                      wy_s.at[k, 0], wy_r.at[k, 0], dev(x, yo(1), z, c)))
        hi = go(rcopy(wp.at[sh, pl.ds(240, 240)], wp.at[sh, pl.ds(240, 240)],
                      wy_s.at[k, 1], wy_r.at[k, 1], dev(x, yo(NY - 1), z, c)))
        return lo, hi

    def fwd_c(k, j):
        sh = shard(k, yl if j == 0 else 1 - yl, c)
        return go(rcopy(wp.at[sh], wp.at[sh], wc_s.at[k, j], wc_r.at[k, j], dev(x, y, z, oc)))

    wy = {0: fwd_y(0)}
    wc = {(0, 0): fwd_c(0, 0)}

    def rows(i, carry):
        r0 = pl.multiple_of(i * 16, 16)
        acc = jnp.zeros((16, 128), F32)
        for j in range(D // 128):
            v = h[pl.ds(r0, 16), j * 128:(j + 1) * 128].astype(F32)
            acc = acc + v * v
        ms = jnp.sum(acc, axis=1, keepdims=True) * (1.0 / D)
        r = jnp.broadcast_to(lax.rsqrt(ms + 1e-05), (16, 128))
        rv[pl.ds(r0, 16), :] = r
        for j in range(D // 128):
            v = h[pl.ds(r0, 16), j * 128:(j + 1) * 128].astype(F32)
            gj = gain[:, j * 128:(j + 1) * 128]
            s[pl.ds(r0, 16), j * 128:(j + 1) * 128] = ((v * r) * gj).astype(BF16)
        return carry

    def quarter(i):
        hcopies[i].wait()
        lax.fori_loop(6 * i, 6 * i + 6, rows, 0)

    quarter(0)
    quarter(1)
    for n, k in enumerate((1, 3, 2)):
        wx[k].wait_recv()
        wy[k] = fwd_y(k)
        wc[(k, 0)] = fwd_c(k, 0)
        if n < 2:
            quarter(2 + n)

    def unpack(k, j):
        l = yl if j == 0 else 1 - yl
        q = xo(NX - k if k else 0) * 2 + l
        for cc in range(2):
            sh = q * 2 + cc
            wu[q, cc * 320:(cc + 1) * 320, 0:128] = wp[sh, 0:320, :]
            b = wp[sh, 320:480, :]
            wu[q, cc * 320:cc * 320 + 160, 128:256] = b
            wu[q, cc * 320 + 160:(cc + 1) * 320, 128:256] = pltpu.roll(
                b.astype(F32), 64, 1).astype(BF16)
        return q

    def add_logits(k, j):
        wc[(k, j)].wait_recv()
        q = unpack(k, j)
        part = jnp.dot(s[:, pl.ds(pl.multiple_of(q * QW, 128), QW)], wu[q],
                       preferred_element_type=F32)
        if (k, j) == (0, 0):
            logit[...] = part
        else:
            logit[...] += part

    add_logits(0, 0)

    def take_y(k):
        wy[k][0].wait_recv()
        wy[k][1].wait_recv()
        wc[(k, 1)] = fwd_c(k, 1)

    order = (0, 1, 3, 2)
    take_y(0)
    take_y(1)
    add_logits(1, 0)
    add_logits(3, 0)
    take_y(3)
    add_logits(0, 1)
    add_logits(2, 0)
    take_y(2)
    add_logits(1, 1)
    add_logits(3, 1)
    add_logits(2, 1)

    lane = lax.broadcasted_iota(jnp.int32, (TOK, 256), 1)
    lg = jnp.where(lane < V, logit[...], -3e38)
    m = jnp.max(lg, axis=1, keepdims=True)
    e = jnp.where(lane < V, jnp.exp(lg - m), 0.0)
    p = e / jnp.sum(e, axis=1, keepdims=True)
    tc = jnp.concatenate([t_col, t_col], axis=1)
    onehot = (tc == lane.astype(F32)).astype(F32)
    dl = ((p - onehot) * SCALE).astype(BF16)
    dlz[...] = dl
    up = dl[:, 128:256].astype(F32)
    dle[:, 0:128] = dl[:, 0:128]
    dle[:, 128:256] = (up + pltpu.roll(up, 64, 1)).astype(BF16)

    lane_lo = lax.broadcasted_iota(jnp.int32, (320, 128), 1) < 64
    xorder = (1, 3, 2, 0)
    part_dev = dev(x, y, z, oc)

    ac = {}
    bcp = {}
    for k in xorder:
        xx = xo(k)
        for l in range(2):
            q = xx * 2 + l
            wv = lax.dot_general(
                s[:, pl.ds(pl.multiple_of(q * QW, 128), QW)], dle[...],
                (((0,), (0,)), ((), ())), preferred_element_type=F32)
            top, bot = wv[0:320, 0:128], wv[320:640, 0:128]
            a_send[xx, l] = jnp.where(c == 0, bot, top).astype(BF16)
            ac[(k, l)] = go(rcopy(a_send.at[xx, l], a_core.at[xx, l],
                                  ac_s.at[k, l], ac_r.at[k, l], part_dev))
            a_keep[xx, l] = jnp.where(c == 0, top, bot)
            bq = jnp.where(lane_lo, wv[0:320, 128:256], wv[320:640, 128:256])
            b_keep[xx, l] = bq
            b_send[xx, l] = bq.astype(BF16)
            bcp[(k, l)] = rcopy(b_send.at[xx, l], b_core.at[xx, l],
                                bc_s.at[k, l], bc_r.at[k, l], part_dev)

            @pl.when(lax.div(xx, 2) != c)
            def _():
                bcp[(k, l)].start()

    ax = {}
    byc = {}
    for k in xorder:
        xx = xo(k)
        for l in range(2):
            ac[(k, l)].wait_recv()
            tot = a_keep[xx, l] + a_core[xx, l].astype(F32)
            if k:
                ax_send[k - 1, l] = tot.astype(BF16)
                ax[(k, l)] = go(rcopy(ax_send.at[k - 1, l], ax_recv.at[k - 1, l],
                                      ax_s.at[k, l], ax_r.at[k, l], dev(xx, y, z, c)))
            else:
                a_acc[l] = tot
        bi = lax.rem(xx, 2)
        for j in range(1, NY):
            yy = yo(j)
            byc[(k, j)] = rcopy(by_send.at[bi, lax.rem(yy, 2), pl.ds(pl.multiple_of(lax.div(yy, 2) * 80, 16), 80)],
                                by_recv.at[bi, j - 1],
                                by_s.at[bi, j], by_r.at[bi, j], dev(x, yy, z, c))

        @pl.when(lax.div(xx, 2) == c)
        def _():
            for l in range(2):
                bcp[(k, l)].wait_recv()
                tot = b_keep[xx, l] + b_core[xx, l].astype(F32)
                by_acc[bi, l] = tot
                by_send[bi, l] = tot.astype(BF16)
            for j in range(1, NY):
                byc[(k, j)].start()

    def gain_chunk(q, carry):
        cols = pl.ds(pl.multiple_of(q * QW, 128), QW)
        ds = lax.dot_general(dlz[...], wu[q], (((1,), (1,)), ((), ())),
                             preferred_element_type=F32)
        n = h[:, cols].astype(F32) * jnp.concatenate([rv[...]] * 5, axis=1)
        g_loc[pl.ds(q, 1), :] = jnp.sum(ds * n, axis=0, keepdims=True)
        return carry

    lax.fori_loop(0, 8, gain_chunk, 0)
    glane = pl.multiple_of(c * 256, 128)
    golane = pl.multiple_of(oc * 256, 128)
    gc = go(rcopy(g_loc.at[:, pl.ds(golane, 384)], g_core, gc_s, gc_r, part_dev))

    ay = {}
    for l in range(2):
        tot = a_acc[l]
        for k in (1, 3, 2):
            ax[(k, l)].wait_recv()
            tot = tot + ax_recv[k - 1, l].astype(F32)
        a_acc[l] = tot
        ay_send[l] = tot.astype(BF16)
    for j in range(1, NY):
        yy = yo(j)
        ay[j] = go(rcopy(ay_send.at[lax.rem(yy, 2), pl.ds(pl.multiple_of(lax.div(yy, 2) * 80, 16), 80)],
                         ay_recv.at[j - 1], ay_s.at[j], ay_r.at[j], dev(x, yy, z, c)))

    def spread(buf, own, stage_s, stage_r, count, to):
        cps = []
        for k in range(1, count):
            cps.append(go(rcopy(buf.at[own], buf.at[own], stage_s.at[k], stage_r.at[k], to(k))))
        return cps

    gc.wait_recv()
    g_x[x] = g_loc[:, pl.ds(glane, 384)] + g_core[...]
    gx = spread(g_x, x, gx_s, gx_r, NX, lambda k: dev(xo(k), y, z, c))

    for b in range(2):
        tot = by_acc[b, yl, pl.ds(pl.multiple_of(yh * 80, 16), 80)]
        for j in range(1, NY):
            pltpu.make_async_copy(by_recv.at[b, j - 1], by_recv.at[b, j - 1], by_r.at[b, j]).wait()
            tot = tot + by_recv[b, j - 1].astype(F32)
        bx_send[b] = tot
    mine = lax.div(x, 2) == c
    bx = {}
    for k in range(1, NX):
        xx = xo(k)
        bx[k] = rcopy(bx_send.at[lax.rem(xx, 2)], bx_recv.at[k - 1],
                      bx_s.at[k], bx_r.at[k], dev(xx, y, z, c))

        @pl.when(lax.div(xx, 2) == c)
        def _():
            bx[k].start()

    for cp in gx:
        cp.wait_recv()
    g_y[y] = (g_x[0] + g_x[1]) + (g_x[2] + g_x[3])
    gy = spread(g_y, y, gy_s, gy_r, NY, lambda k: dev(x, yo(k), z, c))

    tot = a_acc[yl, pl.ds(pl.multiple_of(yh * 80, 16), 80)]
    for j in range(1, NY):
        ay[j].wait_recv()
        tot = tot + ay_recv[j - 1].astype(F32)
    a_fin[0:80] = tot
    for i in range(NZ):
        az_send[i] = a_fin[10 * i:10 * i + 16]
    az = {}
    for k in range(1, NZ):
        zz = zo(k)
        az[k] = go(rcopy(az_send.at[zz], az_recv.at[k], az_s.at[k], az_r.at[k], dev(x, y, zz, c)))

    bz = {}
    for k in range(NZ):
        zz = zo(k)
        for o in range(0 if k else 1, 2):
            bz[(k, o)] = rcopy(bz_send.at[zz], bz_recv.at[k], bz_s.at[k, o], bz_r.at[k],
                               dev(x, y, zz, c if o == 0 else oc))

    @pl.when(mine)
    def _():
        t = bx_send[lax.rem(x, 2)]
        for k in (1, 3, 2):
            bx[k].wait_recv()
            t = t + bx_recv[k - 1]
        b_fin[0:80] = t
        for i in range(NZ):
            bz_send[i] = b_fin[10 * i:10 * i + 16]
        bz_recv[0] = bz_send[z]
        for k in range(NZ):
            for o in range(0 if k else 1, 2):
                bz[(k, o)].start()

    for cp in gy:
        cp.wait_recv()
    g_z[z] = ((g_y[0] + g_y[1]) + (g_y[2] + g_y[3])) + ((g_y[4] + g_y[5]) + (g_y[6] + g_y[7]))
    gz = spread(g_z, z, gz_s, gz_r, NZ, lambda k: dev(x, y, zo(k), c))

    ta = az_send[z]
    for k in range(1, NZ):
        az[k].wait_recv()
        ta = ta + az_recv[k]
    wg_out[:, 0:128] = ta[0:10]

    @pl.when(jnp.logical_not(mine))
    def _():
        bz[(0, 1)].wait_recv()

    tb = bz_recv[0]
    for k in range(1, NZ):
        bz[(k, 0)].wait_recv()
        tb = tb + bz_recv[k]
    tb = jnp.where(c == 0, tb, pltpu.roll(tb, 64, 1))
    wg_out[:, 128:192] = tb[0:10, 0:64]

    for cp in gz:
        cp.wait_recv()
    g_mine[...] = ((g_z[0] + g_z[1]) + (g_z[2] + g_z[3])) + ((g_z[4] + g_z[5]) + (g_z[6] + g_z[7]))
    gf = go(rcopy(g_mine, g_full, gf_s, gf_r, part_dev))
    gf.wait_recv()

    @pl.when(c == 0)
    def _():
        gg_out[:, 0:384] = g_mine[...]
        gg_out[:, 384:640] = g_full[:, 128:384]

    @pl.when(c == 1)
    def _():
        gg_out[:, 0:256] = g_full[:, 0:256]
        gg_out[:, 256:640] = g_mine[...]

    for cp in started:
        cp.wait_send()
    for k in range(NX):
        xx = xo(k)

        @pl.when(lax.div(xx, 2) != c)
        def _():
            for l in range(2):
                bcp[(k, l)].wait_send()

        @pl.when(lax.div(xx, 2) == c)
        def _():
            for j in range(1, NY):
                byc[(k, j)].wait_send()
            if k:
                bx[k].wait_send()

    @pl.when(mine)
    def _():
        for k in range(NZ):
            for o in range(0 if k else 1, 2):
                bz[(k, o)].wait_send()


def on_device(hidden, targets, head_weight, norm_gain):
    dma = pltpu.SemaphoreType.DMA
    vm = pltpu.VMEM
    scratch = [
        vm((TOK, D), BF16), vm((TOK, D), BF16), vm((TOK, 128), F32),
        vm((16, 480, 128), BF16), vm((8, QW, 256), BF16),
        vm((TOK, 256), F32), vm((TOK, 256), BF16), vm((TOK, 256), BF16),
        vm((4, 2, 320, 128), F32), vm((4, 2, 320, 128), BF16), vm((4, 2, 320, 128), BF16),
        vm((4, 2, 320, 128), F32), vm((4, 2, 320, 128), BF16), vm((4, 2, 320, 128), BF16),
        vm((3, 2, 320, 128), BF16), vm((3, 2, 320, 128), BF16), vm((2, 320, 128), F32),
        vm((2, 320, 128), BF16), vm((7, 80, 128), BF16),
        vm((96, 128), F32), vm((8, 16, 128), F32), vm((8, 16, 128), F32),
        vm((2, 2, 320, 128), BF16), vm((2, 2, 320, 128), F32), vm((2, 7, 80, 128), BF16),
        vm((2, 80, 128), F32), vm((3, 80, 128), F32),
        vm((96, 128), F32), vm((8, 16, 128), F32), vm((8, 16, 128), F32),
        vm((8, QW), F32), vm((8, 384), F32), vm((4, 8, 384), F32),
        vm((8, 8, 384), F32), vm((8, 8, 384), F32), vm((8, 384), F32), vm((8, 384), F32),
        dma((4,)),
        dma((4,)), dma((4,)), dma((4, 2)), dma((4, 2)), dma((4, 2)), dma((4, 2)),
        dma((4, 2)), dma((4, 2)), dma((4, 2)), dma((4, 2)),
        dma((4, 2)), dma((4, 2)), dma((8,)), dma((8,)), dma((8,)), dma((8,)),
        dma((2, 8)), dma((2, 8)), dma((4,)), dma((4,)), dma((8, 2)), dma((8,)),
        dma, dma, dma((4,)), dma((4,)), dma((8,)), dma((8,)), dma((8,)), dma((8,)), dma, dma,
    ]
    vspec = pl.BlockSpec(memory_space=pltpu.VMEM)
    wg, gg = pl.pallas_call(
        kernel,
        out_shape=(jax.ShapeDtypeStruct((10, V), F32), jax.ShapeDtypeStruct((8, QW), F32)),
        in_specs=[pl.BlockSpec(memory_space=pl.ANY), vspec, vspec, vspec],
        out_specs=(vspec, vspec),
        scratch_shapes=scratch,
        compiler_params=pltpu.CompilerParams(
            collective_id=0, has_side_effects=True, vmem_limit_bytes=56 * 1024 * 1024),
        cost_estimate=pl.CostEstimate(flops=3 * 2 * TOK * D * V, bytes_accessed=TOK * D * 2,
                                      transcendentals=TOK * V),
    )(hidden, targets.reshape(1, TOK), head_weight, norm_gain.reshape(1, D))
    return wg, gg.reshape(D)


def solution(mesh):
    placed = (P(("section", "dp"), None), P(("section", "dp")), P("section", None), P())
    return jax.shard_map(
        on_device,
        mesh=mesh,
        in_specs=placed,
        out_specs=(P(("section", "dp"), None), P()),
        check_vma=False,
    )
```

```python
import jax
import jax.numpy as jnp
from jax import lax
from jax.experimental import pallas as pl
from jax.experimental.pallas import tpu as pltpu
from jax.sharding import PartitionSpec as P

D = 5120
V = 192
TOK = 384
NX, NY, NZ = 4, 8, 8
QW = 640
MESH = pl.DeviceIdType.MESH
F32 = jnp.float32
BF16 = jnp.bfloat16
SCALE = 1.0 / TOK**0.5


def kernel(
    hid, tgt, wt, gain, wg_out, gg_out,
    h, s, rv, wp, wu, logit, dlz, dle,
    a_keep, a_send, a_core, b_keep, b_send, b_core,
    ax_send, ax_recv, a_acc, ay_send, ay_recv, a_fin, az_send, az_recv,
    bf_send, bf_acc, bf_recv, bx_send, bx_recv, b_fin, bz_send, bz_recv,
    g_loc, g_core, g_x, g_y, g_z, g_mine, g_full,
    hsem,
    wx_s, wx_r, wy_s, wy_r, wc_s, wc_r,
    ac_s, ac_r, bc_s, bc_r,
    ax_s, ax_r, ay_s, ay_r, az_s, az_r,
    bf_s, bf_r, bx_s, bx_r, bz_s, bz_r,
    gc_s, gc_r, gx_s, gx_r, gy_s, gy_r, gz_s, gz_r, gf_s, gf_r,
):
    sec = lax.axis_index("section")
    dp = lax.axis_index("dp")
    c = lax.rem(sec, 2)
    yl = lax.rem(lax.div(sec, 2), 2)
    x = lax.div(sec, 4)
    yh = lax.div(dp, NZ)
    z = lax.rem(dp, NZ)
    y = yh * 2 + yl
    oc = 1 - c
    odd = lax.rem(x, 2)
    mine = lax.div(x, 2) == c

    def dev(x_, y_, z_, c_):
        return (x_ * 4 + lax.rem(y_, 2) * 2 + c_, lax.div(y_, 2) * NZ + z_)

    def xo(k):
        return lax.rem(x + k, NX)

    def yo(k):
        return lax.rem(y + k, NY)

    def zo(k):
        return lax.rem(z + k, NZ)

    def rcopy(src, dst, ss, rs, to):
        return pltpu.make_async_remote_copy(
            src_ref=src, dst_ref=dst, send_sem=ss, recv_sem=rs,
            device_id=to, device_id_type=MESH)

    hcopies = [
        pltpu.make_async_copy(hid.at[pl.ds(96 * i, 96)], h.at[pl.ds(96 * i, 96)], hsem.at[i])
        for i in range(4)
    ]
    for cp in hcopies:
        cp.start()

    barrier = pltpu.get_barrier_semaphore()
    peers = [dev(x, y, z, oc)]
    peers += [dev(xo(k), y, z, c) for k in range(1, NX)]
    peers += [dev(x, yo(k), z, c) for k in range(1, NY)]
    peers += [dev(x, y, zo(k), c) for k in range(1, NZ)]
    for p in peers:
        pl.semaphore_signal(barrier, inc=1, device_id=p, device_id_type=MESH)

    eye = (lax.broadcasted_iota(jnp.int32, (320, 320), 0)
           == lax.broadcasted_iota(jnp.int32, (320, 320), 1)).astype(BF16)
    w = lax.dot_general(eye, wt[...], (((1,), (1,)), ((), ())), preferred_element_type=F32)
    wp[sec, 0:320, :] = w[:, 0:128].astype(BF16)
    wp[sec, 320:480, :] = jnp.concatenate(
        [w[0:160, 128:192], w[160:320, 128:192]], axis=1).astype(BF16)

    pl.semaphore_wait(barrier, len(peers))

    started = []

    def go(cp):
        cp.start()
        started.append(cp)
        return cp

    def shard(k, l, cc):
        return xo(NX - k if k else 0) * 4 + l * 2 + cc

    def half(sh, i):
        return wp.at[sh, pl.ds(240 * i, 240)]

    wx, wy, wc = {}, {}, {}

    def send_x(k, i):
        wx[(k, i)] = go(rcopy(half(sec, i), half(sec, i), wx_s.at[k, i], wx_r.at[k, i],
                              dev(xo(k), y, z, c)))

    def fwd_y(k, i):
        sh = shard(k, yl, c)
        wy[(k, i)] = go(rcopy(half(sh, i), half(sh, i), wy_s.at[k, i], wy_r.at[k, i],
                              dev(x, yo(NY - 1 if i else 1), z, c)))

    def fwd_c(k, j):
        sh = shard(k, yl if j == 0 else 1 - yl, c)
        wc[(k, j)] = go(rcopy(wp.at[sh], wp.at[sh], wc_s.at[k, j], wc_r.at[k, j], dev(x, y, z, oc)))

    for i in range(2):
        send_x(1, i)
        send_x(3, 1 - i)
        fwd_y(0, i)
    fwd_c(0, 0)

    def rows(i, carry):
        r0 = pl.multiple_of(i * 16, 16)
        acc = jnp.zeros((16, 128), F32)
        for j in range(D // 128):
            v = h[pl.ds(r0, 16), j * 128:(j + 1) * 128].astype(F32)
            acc = acc + v * v
        ms = jnp.sum(acc, axis=1, keepdims=True) * (1.0 / D)
        r = jnp.broadcast_to(lax.rsqrt(ms + 1e-05), (16, 128))
        rv[pl.ds(r0, 16), :] = r
        for j in range(D // 128):
            v = h[pl.ds(r0, 16), j * 128:(j + 1) * 128].astype(F32)
            gj = gain[:, j * 128:(j + 1) * 128]
            s[pl.ds(r0, 16), j * 128:(j + 1) * 128] = ((v * r) * gj).astype(BF16)
        return carry

    def quarter(i):
        hcopies[i].wait()
        lax.fori_loop(6 * i, 6 * i + 6, rows, 0)

    def take_x(k, i):
        wx[(k, i)].wait_recv()
        fwd_y(k, i)

    def take_y(k):
        wy[(k, 0)].wait_recv()
        wy[(k, 1)].wait_recv()
        fwd_c(k, 1)

    def unpack(k, j):
        l = yl if j == 0 else 1 - yl
        q = xo(NX - k if k else 0) * 2 + l
        for cc in range(2):
            sh = q * 2 + cc
            wu[q, cc * 320:(cc + 1) * 320, 0:128] = wp[sh, 0:320, :]
            b = wp[sh, 320:480, :]
            wu[q, cc * 320:cc * 320 + 160, 128:256] = b
            wu[q, cc * 320 + 160:(cc + 1) * 320, 128:256] = pltpu.roll(
                b.astype(F32), 64, 1).astype(BF16)
        return q

    def add_logits(k, j):
        wc[(k, j)].wait_recv()
        q = unpack(k, j)
        part = jnp.dot(s[:, pl.ds(pl.multiple_of(q * QW, 128), QW)], wu[q],
                       preferred_element_type=F32)
        if (k, j) == (0, 0):
            logit[...] = part
        else:
            logit[...] += part

    quarter(0)
    for i in range(2):
        send_x(2, i)
    quarter(1)
    quarter(2)
    take_x(1, 0)
    take_x(3, 1)
    quarter(3)
    take_x(1, 1)
    take_x(3, 0)
    fwd_c(1, 0)
    fwd_c(3, 0)
    add_logits(0, 0)
    take_y(0)
    add_logits(1, 0)
    add_logits(3, 0)
    add_logits(0, 1)
    take_x(2, 0)
    take_x(2, 1)
    fwd_c(2, 0)
    add_logits(2, 0)
    take_y(1)
    take_y(3)
    add_logits(1, 1)
    add_logits(3, 1)
    take_y(2)
    add_logits(2, 1)

    lane = lax.broadcasted_iota(jnp.int32, (TOK, 256), 1)
    t_col = jnp.transpose(jnp.broadcast_to(tgt[...].reshape(1, TOK).astype(F32), (128, TOK)))
    tc = jnp.concatenate([t_col, t_col], axis=1)
    onehot = (tc == lane.astype(F32)).astype(F32)
    lg = jnp.where(lane < V, logit[...], -3e38)
    m = jnp.max(lg, axis=1, keepdims=True)
    e = jnp.where(lane < V, jnp.exp(lg - m), 0.0)
    p = e / jnp.sum(e, axis=1, keepdims=True)
    dl = ((p - onehot) * SCALE).astype(BF16)
    dlz[...] = dl
    up = dl[:, 128:256].astype(F32)
    dle[:, 0:128] = dl[:, 0:128]
    dle[:, 128:256] = (up + pltpu.roll(up, 64, 1)).astype(BF16)

    lane_lo = lax.broadcasted_iota(jnp.int32, (320, 128), 1) < 64
    part_dev = dev(x, y, z, oc)

    ac, bcp, ax = {}, {}, {}

    def chunk(l, k):
        xx = xo(k)
        q = xx * 2 + l
        wv = lax.dot_general(
            s[:, pl.ds(pl.multiple_of(q * QW, 128), QW)], dle[...],
            (((0,), (0,)), ((), ())), preferred_element_type=F32)
        top, bot = wv[0:320, 0:128], wv[320:640, 0:128]
        a_send[xx, l] = jnp.where(c == 0, bot, top).astype(BF16)
        ac[(k, l)] = go(rcopy(a_send.at[xx, l], a_core.at[xx, l],
                              ac_s.at[k, l], ac_r.at[k, l], part_dev))
        bq = jnp.where(lane_lo, wv[0:320, 128:256], wv[320:640, 128:256])
        b_send[xx, l] = bq.astype(BF16)
        bcp[(k, l)] = rcopy(b_send.at[xx, l], b_core.at[xx, l],
                            bc_s.at[k, l], bc_r.at[k, l], part_dev)

        @pl.when(lax.div(xx, 2) != c)
        def _():
            bcp[(k, l)].start()

        a_keep[xx, l] = jnp.where(c == 0, top, bot)
        b_keep[xx, l] = bq

    def chip_sum(l, k):
        xx = xo(k)
        ac[(k, l)].wait_recv()
        tot = a_keep[xx, l] + a_core[xx, l].astype(F32)
        if k:
            ax_send[k - 1, l] = tot.astype(BF16)
            ax[(k, l)] = go(rcopy(ax_send.at[k - 1, l], ax_recv.at[k - 1, l],
                                  ax_s.at[k, l], ax_r.at[k, l], dev(xx, y, z, c)))
        else:
            a_acc[l] = tot
        b = lax.rem(xx, 2)
        at = jnp.where(b == 0, y, z)

        @pl.when(lax.div(xx, 2) == c)
        def _():
            bcp[(k, l)].wait_recv()
            tot = b_keep[xx, l] + b_core[xx, l].astype(F32)
            bf_acc[b, l] = tot
            bf_send[b, l] = tot.astype(BF16)
            for i in range(4):
                g = i * 2 + l
                j = lax.rem(g + 8 - at, 8)

                @pl.when(j != 0)
                def _():
                    rcopy(bf_send.at[b, l, pl.ds(80 * i, 80)], bf_recv.at[b, j],
                          bf_s.at[b, j], bf_r.at[b, j],
                          dev(x, jnp.where(b == 0, g, y), jnp.where(b == 0, z, g), c)).start()

    before = None
    for l in range(2):
        for k in (2, 1, 3, 0):
            chunk(l, k)
            if before:
                chip_sum(*before)
            before = (l, k)
    chip_sum(*before)

    def gain_chunk(q, carry):
        cols = pl.ds(pl.multiple_of(q * QW, 128), QW)
        ds = lax.dot_general(dlz[...], wu[q], (((1,), (1,)), ((), ())),
                             preferred_element_type=F32)
        n = h[:, cols].astype(F32) * jnp.concatenate([rv[...]] * 5, axis=1)
        t = jnp.sum(ds * n, axis=0, keepdims=True)
        for i in range(5):
            g_loc[pl.ds(q * 5 + i, 1), :] = t[:, i * 128:(i + 1) * 128]
        return carry

    lax.fori_loop(0, 8, gain_chunk, 0)
    grow = pl.multiple_of(c * 16, 8)
    gorow = pl.multiple_of(oc * 16, 8)
    gc = go(rcopy(g_loc.at[pl.ds(gorow, 24)], g_core, gc_s, gc_r, part_dev))

    ay = {}

    def x_to_y(l):
        tot = a_acc[l]
        for k in (1, 3, 2):
            ax[(k, l)].wait_recv()
            tot = tot + ax_recv[k - 1, l].astype(F32)
        a_acc[l] = tot
        ay_send[l] = tot.astype(BF16)
        for i in range(4):
            g = i * 2 + l
            j = lax.rem(g + 8 - y, 8)

            @pl.when(j != 0)
            def _():
                rcopy(ay_send.at[l, pl.ds(80 * i, 80)], ay_recv.at[j],
                      ay_s.at[j], ay_r.at[j], dev(x, g, z, c)).start()

    def spread(buf, own, stage_s, stage_r, count, to):
        cps = []
        for k in range(1, count):
            cps.append(go(rcopy(buf.at[own], buf.at[own], stage_s.at[k], stage_r.at[k], to(k))))
        return cps

    def sum8(v):
        return ((v[0] + v[1]) + (v[2] + v[3])) + ((v[4] + v[5]) + (v[6] + v[7]))

    x_to_y(0)

    gc.wait_recv()
    g_x[x] = g_loc[pl.ds(grow, 24)] + g_core[...]
    gx = spread(g_x, x, gx_s, gx_r, NX, lambda k: dev(xo(k), y, z, c))

    x_to_y(1)

    for cp in gx:
        cp.wait_recv()
    g_z[z] = (g_x[0] + g_x[1]) + (g_x[2] + g_x[3])
    gz = spread(g_z, z, gz_s, gz_r, NZ, lambda k: dev(x, y, zo(k), c))

    for b in range(2):
        at = z if b else y
        tot = bf_acc[b, lax.rem(at, 2), pl.ds(pl.multiple_of(lax.div(at, 2) * 80, 16), 80)]
        for j in range(1, 8):
            rcopy(bf_recv.at[b, j], bf_recv.at[b, j], bf_s.at[b, j], bf_r.at[b, j],
                  part_dev).wait_recv()
            tot = tot + bf_recv[b, j].astype(F32)
        bx_send[b] = tot
    bx = {}
    for k in range(1, NX):
        xx = xo(k)
        bx[k] = rcopy(bx_send.at[lax.rem(xx, 2)], bx_recv.at[k - 1],
                      bx_s.at[k], bx_r.at[k], dev(xx, y, z, c))

        @pl.when(lax.div(xx, 2) == c)
        def _():
            bx[k].start()

    for cp in gz:
        cp.wait_recv()
    g_y[y] = sum8(g_z)
    gy = spread(g_y, y, gy_s, gy_r, NY, lambda k: dev(x, yo(k), z, c))

    tot = a_acc[yl, pl.ds(pl.multiple_of(yh * 80, 16), 80)]
    for j in range(1, NY):
        rcopy(ay_recv.at[j], ay_recv.at[j], ay_s.at[j], ay_r.at[j], part_dev).wait_recv()
        tot = tot + ay_recv[j].astype(F32)
    a_fin[0:80] = tot
    for i in range(NZ):
        az_send[i] = a_fin[10 * i:10 * i + 16]
    az = {}
    for k in range(1, NZ):
        zz = zo(k)
        az[k] = go(rcopy(az_send.at[zz], az_recv.at[k], az_s.at[k], az_r.at[k], dev(x, y, zz, c)))

    yd = jnp.where(odd == 1, z, y)
    slot = jnp.where(odd == 1, y, z)
    bz = {}
    for k in range(NZ):
        zz = zo(k)
        for o in range(2):
            bz[(k, o)] = rcopy(bz_send.at[zz], bz_recv.at[slot], bz_s.at[k, o], bz_r.at[slot],
                               dev(x, yd, zz, oc if o else c))

    @pl.when(mine)
    def _():
        t = bx_send[odd]
        for k in (1, 3, 2):
            bx[k].wait_recv()
            t = t + bx_recv[k - 1]
        b_fin[0:80] = t
        for i in range(NZ):
            bz_send[i] = b_fin[10 * i:10 * i + 16]

        @pl.when(yd == y)
        def _():
            bz_recv[slot] = bz_send[z]

        @pl.when(yd != y)
        def _():
            bz[(0, 0)].start()

        for k in range(NZ):
            for o in range(0 if k else 1, 2):
                bz[(k, o)].start()

    for cp in gy:
        cp.wait_recv()
    g_mine[...] = sum8(g_y)
    gf = go(rcopy(g_mine, g_full, gf_s, gf_r, part_dev))

    ta = az_send[z]
    for k in range(1, NZ):
        az[k].wait_recv()
        ta = ta + az_recv[k]
    wg_out[:, 0:128] = ta[0:10]

    for i in range(NZ):
        local = jnp.logical_and(jnp.logical_and(mine, yd == y), slot == i)

        @pl.when(jnp.logical_not(local))
        def _():
            rcopy(bz_recv.at[i], bz_recv.at[i], bz_s.at[0, 0], bz_r.at[i], part_dev).wait_recv()

    tb = sum8(bz_recv)
    tb = jnp.where(c == 0, tb, pltpu.roll(tb, 64, 1))
    wg_out[:, 128:192] = tb[0:10, 0:64]

    gf.wait_recv()

    @pl.when(c == 0)
    def _():
        gg_out[0:24] = g_mine[...]
        gg_out[24:40] = g_full[8:24]

    @pl.when(c == 1)
    def _():
        gg_out[0:16] = g_full[0:16]
        gg_out[16:40] = g_mine[...]

    for cp in started:
        cp.wait_send()
    for j in range(1, 8):
        rcopy(ay_recv.at[j], ay_recv.at[j], ay_s.at[j], ay_r.at[j], part_dev).wait_send()
        for b in range(2):
            rcopy(bf_recv.at[b, j], bf_recv.at[b, j], bf_s.at[b, j], bf_r.at[b, j],
                  part_dev).wait_send()
    for k in range(NX):
        xx = xo(k)

        @pl.when(lax.div(xx, 2) != c)
        def _():
            for l in range(2):
                bcp[(k, l)].wait_send()

        if k:
            @pl.when(lax.div(xx, 2) == c)
            def _():
                bx[k].wait_send()

    @pl.when(mine)
    def _():
        @pl.when(yd != y)
        def _():
            bz[(0, 0)].wait_send()

        for k in range(NZ):
            for o in range(0 if k else 1, 2):
                bz[(k, o)].wait_send()


def leave(wg_in, gg_in, wg_out, gg_out):
    wg_out[...] = wg_in[...]
    gg_out[...] = gg_in[...]


def on_device(hidden, targets, head_weight, norm_gain):
    dma = pltpu.SemaphoreType.DMA
    vm = pltpu.VMEM
    scratch = [
        vm((TOK, D), BF16), vm((TOK, D), BF16), vm((TOK, 128), F32),
        vm((16, 480, 128), BF16), vm((8, QW, 256), BF16),
        vm((TOK, 256), F32), vm((TOK, 256), BF16), vm((TOK, 256), BF16),
        vm((4, 2, 320, 128), F32), vm((4, 2, 320, 128), BF16), vm((4, 2, 320, 128), BF16),
        vm((4, 2, 320, 128), F32), vm((4, 2, 320, 128), BF16), vm((4, 2, 320, 128), BF16),
        vm((3, 2, 320, 128), BF16), vm((3, 2, 320, 128), BF16), vm((2, 320, 128), F32),
        vm((2, 320, 128), BF16), vm((8, 80, 128), BF16),
        vm((96, 128), F32), vm((8, 16, 128), F32), vm((8, 16, 128), F32),
        vm((2, 2, 320, 128), BF16), vm((2, 2, 320, 128), F32), vm((2, 8, 80, 128), BF16),
        vm((2, 80, 128), F32), vm((3, 80, 128), F32),
        vm((96, 128), F32), vm((8, 16, 128), F32), vm((8, 16, 128), F32),
        vm((40, 128), F32), vm((24, 128), F32), vm((4, 24, 128), F32),
        vm((8, 24, 128), F32), vm((8, 24, 128), F32), vm((24, 128), F32), vm((24, 128), F32),
        dma((4,)),
        dma((4, 2)), dma((4, 2)), dma((4, 2)), dma((4, 2)), dma((4, 2)), dma((4, 2)),
        dma((4, 2)), dma((4, 2)), dma((4, 2)), dma((4, 2)),
        dma((4, 2)), dma((4, 2)), dma((8,)), dma((8,)), dma((8,)), dma((8,)),
        dma((2, 8)), dma((2, 8)), dma((4,)), dma((4,)), dma((8, 2)), dma((8,)),
        dma, dma, dma((4,)), dma((4,)), dma((8,)), dma((8,)), dma((8,)), dma((8,)), dma, dma,
    ]
    vspec = pl.BlockSpec(memory_space=pltpu.VMEM)
    outs = (jax.ShapeDtypeStruct((10, V), F32), jax.ShapeDtypeStruct((40, 128), F32))
    wg, gg = pl.pallas_call(
        kernel,
        out_shape=outs,
        in_specs=[pl.BlockSpec(memory_space=pl.ANY), vspec, vspec, vspec],
        out_specs=(vspec, vspec),
        scratch_shapes=scratch,
        compiler_params=pltpu.CompilerParams(
            collective_id=0, has_side_effects=True, vmem_limit_bytes=56 * 1024 * 1024),
        cost_estimate=pl.CostEstimate(flops=3 * 2 * TOK * D * V, bytes_accessed=TOK * D * 2,
                                      transcendentals=TOK * V),
    )(hidden, targets, head_weight.T, norm_gain.reshape(1, D))
    wg, gg = pl.pallas_call(
        leave, out_shape=outs, in_specs=[vspec, vspec], out_specs=(vspec, vspec),
    )(wg, gg)
    return wg, gg.reshape(D)


def solution(mesh):
    placed = (P(("section", "dp"), None), P(("section", "dp")), P("section", None), P())
    return jax.shard_map(
        on_device,
        mesh=mesh,
        in_specs=placed,
        out_specs=(P(("section", "dp"), None), P()),
        check_vma=False,
    )
```

```python
import jax
import jax.numpy as jnp
from jax import lax
from jax.experimental import pallas as pl
from jax.experimental.pallas import tpu as pltpu
from jax.sharding import PartitionSpec as P

D = 5120
V = 192
TOK = 384
NX, NY, NZ = 4, 8, 8
QW = 640
MESH = pl.DeviceIdType.MESH
F32 = jnp.float32
BF16 = jnp.bfloat16
SCALE = 1.0 / TOK**0.5


def kernel(
    hid, tgt_in, wt_in, gain_in, wg_out, gg_out,
    tgt, wt, gain, h, s, wp, wu, logit, dle,
    a_keep, a_send, a_core, b_keep, b_send, b_core,
    ax_send, ax_recv, a_pend, a_acc,
    ay_send, ay_recv, a1_p32, a1_p16, a1_recv, a_fin0, a_fin1, az0_send, az1_send, az_recv,
    b0_send, b0_acc, b0_recv, b1_acc, b1_p32, b1_p16, b1_recv,
    bx_send, bx_recv, b_fin, bz_send, bz_recv,
    g_loc, g_core, g_x, g_y, g_z, g_mine, g_full,
    hsem,
    wx_s, wx_r, wy_s, wy_r, wc_s, wc_r, ac_s, ac_r, bc_s, bc_r,
    ax_s, axr_r, ax_r, ay_s, ay_r, a1_s, a1_r, az_s, az_r,
    b0_s, b0_r, b1_s, b1_r, bx_s, bx_r, bz_s, bz_r,
    gc_s, gc_r, gx_s, gx_r, gy_s, gy_r, gz_s, gz_r, gf_s, gf_r,
):
    sec = lax.axis_index("section")
    dp = lax.axis_index("dp")
    c = lax.rem(sec, 2)
    yl = lax.rem(lax.div(sec, 2), 2)
    x = lax.div(sec, 4)
    yh = lax.div(dp, NZ)
    z = lax.rem(dp, NZ)
    y = yh * 2 + yl
    oc = 1 - c
    odd = lax.rem(x, 2)
    mine = lax.div(x, 2) == c

    def dev(x_, y_, z_, c_):
        return (x_ * 4 + lax.rem(y_, 2) * 2 + c_, lax.div(y_, 2) * NZ + z_)

    def xo(k):
        return lax.rem(x + k, NX)

    def yo(k):
        return lax.rem(y + k, NY)

    def zo(k):
        return lax.rem(z + k, NZ)

    def rcopy(src, dst, ss, rs, to):
        return pltpu.make_async_remote_copy(
            src_ref=src, dst_ref=dst, send_sem=ss, recv_sem=rs,
            device_id=to, device_id_type=MESH)

    barrier = pltpu.get_barrier_semaphore()
    peers = [dev(x, y, z, oc)]
    peers += [dev(xo(k), y, z, c) for k in range(1, NX)]
    peers += [dev(x, yo(k), z, c) for k in range(1, NY)]
    peers += [dev(x, y, zo(k), c) for k in range(1, NZ)]
    for p in peers:
        pl.semaphore_signal(barrier, inc=1, device_id=p, device_id_type=MESH)

    def fetch(src, dst, i):
        cp = pltpu.make_async_copy(src, dst, hsem.at[i])
        cp.start()
        return cp

    wcopy = fetch(wt_in, wt, 4)
    hcopies = [fetch(hid.at[pl.ds(96 * i, 96)], h.at[pl.ds(96 * i, 96)], i) for i in range(4)]
    gcopy = fetch(gain_in, gain, 5)
    tcopy = fetch(tgt_in, tgt, 6)

    eye = (lax.broadcasted_iota(jnp.int32, (320, 320), 0)
           == lax.broadcasted_iota(jnp.int32, (320, 320), 1)).astype(BF16)
    wcopy.wait()
    w = lax.dot_general(eye, wt[...], (((1,), (1,)), ((), ())), preferred_element_type=F32)
    wp[sec, 0:320, :] = w[:, 0:128].astype(BF16)
    wp[sec, 320:480, :] = jnp.concatenate(
        [w[0:160, 128:192], w[160:320, 128:192]], axis=1).astype(BF16)

    pl.semaphore_wait(barrier, len(peers))

    def go(cp):
        cp.start()
        return cp

    def got(ref, rs):
        rcopy(ref, ref, gf_s, rs, dev(x, y, z, oc)).wait_recv()

    def sent(ref, ss):
        rcopy(ref, ref, ss, gf_r, dev(x, y, z, oc)).wait_send()

    def shard(k, l, cc):
        return xo(NX - k if k else 0) * 4 + l * 2 + cc

    def half(sh, i):
        return wp.at[sh, pl.ds(240 * i, 240)]

    wx, wc = {}, {}

    def send_x(k, i):
        wx[(k, i)] = go(rcopy(half(sec, i), half(sec, i), wx_s, wx_r.at[k - 1, i],
                              dev(xo(k), y, z, c)))

    def fwd_y(k, i):
        sh = shard(k, yl, c)
        go(rcopy(half(sh, i), half(sh, i), wy_s, wy_r.at[k], dev(x, yo(NY - 1 if i else 1), z, c)))

    def fwd_c(k, j):
        sh = shard(k, yl if j == 0 else 1 - yl, c)
        wc[(k, j)] = go(rcopy(wp.at[sh], wp.at[sh], wc_s, wc_r.at[k, j], dev(x, y, z, oc)))

    send_x(1, 0)
    send_x(3, 1)
    fwd_y(0, 0)
    fwd_y(0, 1)
    send_x(1, 1)
    send_x(3, 0)
    fwd_c(0, 0)

    def rows(i, carry):
        r0 = pl.multiple_of(i * 16, 16)
        acc = jnp.zeros((16, 128), F32)
        for j in range(D // 128):
            v = h[pl.ds(r0, 16), j * 128:(j + 1) * 128].astype(F32)
            acc = acc + v * v
        ms = jnp.sum(acc, axis=1, keepdims=True) * (1.0 / D)
        r = jnp.broadcast_to(lax.rsqrt(ms + 1e-05), (16, 128))
        for j in range(D // 128):
            v = h[pl.ds(r0, 16), j * 128:(j + 1) * 128].astype(F32)
            gj = gain[:, j * 128:(j + 1) * 128]
            s[pl.ds(r0, 16), j * 128:(j + 1) * 128] = ((v * r) * gj).astype(BF16)
        return carry

    def block(i):
        if i == 0:
            gcopy.wait()
        if i % 2 == 0:
            hcopies[i // 2].wait()
        lax.fori_loop(3 * i, 3 * i + 3, rows, 0)

    def take_x(k, i):
        wx[(k, i)].wait_recv()
        if (k, i) in ((1, 0), (3, 1)):
            sh = shard(k, yl, c)
            wx[(2, i)] = go(rcopy(half(sh, i), half(sh, i), wx_s, wx_r.at[1, i],
                                  dev(xo(k), y, z, c)))
        fwd_y(k, i)

    def take_y(k):
        got(wp.at[0], wy_r.at[k])
        fwd_c(k, 1)

    def unpack(k, j):
        l = yl if j == 0 else 1 - yl
        q = xo(NX - k if k else 0) * 2 + l
        for cc in range(2):
            sh = q * 2 + cc
            wu[q, cc * 320:(cc + 1) * 320, 0:128] = wp[sh, 0:320, :]
            b = wp[sh, 320:480, :]
            wu[q, cc * 320:cc * 320 + 160, 128:256] = b
            wu[q, cc * 320 + 160:(cc + 1) * 320, 128:256] = pltpu.roll(
                b.astype(F32), 64, 1).astype(BF16)
        return q

    def add_logits(k, j):
        wc[(k, j)].wait_recv()
        q = unpack(k, j)
        part = jnp.dot(s[:, pl.ds(pl.multiple_of(q * QW, 128), QW)], wu[q],
                       preferred_element_type=F32)
        if (k, j) == (0, 0):
            logit[...] = part
        else:
            logit[...] += part

    for i in range(6):
        block(i)
    take_x(1, 0)
    take_x(3, 1)
    block(6)
    block(7)
    take_x(1, 1)
    take_x(3, 0)
    fwd_c(1, 0)
    fwd_c(3, 0)
    take_y(0)
    add_logits(0, 0)
    add_logits(1, 0)
    take_x(2, 0)
    take_x(2, 1)
    fwd_c(2, 0)
    add_logits(3, 0)
    add_logits(0, 1)
    add_logits(2, 0)
    take_y(1)
    take_y(3)
    add_logits(1, 1)
    take_y(2)
    add_logits(3, 1)
    add_logits(2, 1)

    lane = lax.broadcasted_iota(jnp.int32, (TOK, 256), 1)
    tcopy.wait()
    t_col = jnp.transpose(jnp.broadcast_to(tgt[...].reshape(1, TOK).astype(F32), (128, TOK)))
    tc = jnp.concatenate([t_col, t_col], axis=1)
    onehot = (tc == lane.astype(F32)).astype(F32)
    lg = jnp.where(lane < V, logit[...], -3e38)
    m = jnp.max(lg, axis=1, keepdims=True)
    e = jnp.where(lane < V, jnp.exp(lg - m), 0.0)
    p = e / jnp.sum(e, axis=1, keepdims=True)
    dl = ((p - onehot) * SCALE).astype(BF16)
    up = dl[:, 128:256].astype(F32)
    dle[:, 0:128] = dl[:, 0:128]
    dle[:, 128:256] = (up + pltpu.roll(up, 64, 1)).astype(BF16)

    lane_lo = lax.broadcasted_iota(jnp.int32, (320, 128), 1) < 64
    pick_row = lax.broadcasted_iota(jnp.int32, (8, 128), 0)
    pick_half = (lax.broadcasted_iota(jnp.int32, (8, 128), 1) >= 64).astype(jnp.int32)
    ones = jnp.ones((8, 128), BF16)
    halves = (pick_row == pick_half).astype(BF16)
    part_dev = dev(x, y, z, oc)
    g_loc[...] = jnp.zeros((16, 320), F32)

    def chunk(l, k):
        xx = xo(k)
        q = xx * 2 + l
        wv = lax.dot_general(
            s[:, pl.ds(pl.multiple_of(q * QW, 128), QW)], dle[...],
            (((0,), (0,)), ((), ())), preferred_element_type=F32)
        top, bot = wv[0:320, 0:128], wv[320:640, 0:128]
        a_send[xx, l] = jnp.where(c == 0, bot, top).astype(BF16)
        go(rcopy(a_send.at[xx, l], a_core.at[xx, l], ac_s, ac_r.at[k, l], part_dev))
        bq = jnp.where(lane_lo, wv[0:320, 128:256], wv[320:640, 128:256])
        b_send[xx, l] = bq.astype(BF16)

        @pl.when(lax.div(xx, 2) != c)
        def _():
            go(rcopy(b_send.at[xx, l], b_core.at[xx, l], bc_s, bc_r.at[lax.rem(xx, 2), l], part_dev))

        a_keep[xx, l] = jnp.where(c == 0, top, bot)
        b_keep[xx, l] = bq

    def x_send(l, n, v):
        ax_send[l, n] = v.astype(BF16)
        rs = axr_r.at[l, n // 3] if n % 3 == 0 else ax_r.at[l]
        go(rcopy(ax_send.at[l, n], ax_recv.at[l, n], ax_s, rs, dev(xo(1 if n < 3 else 3), y, z, c)))

    def x_relay(l):
        for i in range(2):
            got(ax_recv.at[l, 3 * i], axr_r.at[l, i])
            x_send(l, 3 * i + 2, a_pend[l, i] + ax_recv[l, 3 * i].astype(F32))

    def row_sums(pick, v):
        hi = v.astype(BF16)
        lo = (v - hi.astype(F32)).astype(BF16)
        dims = (((1,), (1,)), ((), ()))
        return (lax.dot_general(pick, hi, dims, preferred_element_type=F32)
                + lax.dot_general(pick, lo, dims, preferred_element_type=F32))

    def by_z(src, dst):
        for j in range(NZ):
            for i in range(4):
                dst[j, 10 * i:10 * i + 16] = src[80 * i + 10 * j:80 * i + 10 * j + 16]

    def chip_sum(l, k):
        xx = xo(k)
        q = xx * 2 + l
        got(a_core.at[0, 0], ac_r.at[k, l])
        tot = a_keep[xx, l] + a_core[xx, l].astype(F32)
        if k == 0:
            a_acc[l, 0:320] = tot
        if k == 1:
            x_send(l, 1, tot[160:320])
            a_pend[l, 0] = tot[0:160]
        if k == 2:
            x_send(l, 0, tot[0:160])
            x_send(l, 3, tot[160:320])
        if k == 3:
            x_send(l, 4, tot[0:160])
            a_pend[l, 1] = tot[160:320]
        wa = wu[q, pl.ds(pl.multiple_of(c * 320, 16), 320), 0:128].astype(F32)
        row = c * 8 + q
        g_loc[pl.ds(row, 1), :] += row_sums(ones, tot * wa)[0:1]

        @pl.when(lax.div(xx, 2) == c)
        def _():
            b = lax.rem(xx, 2)
            got(b_core.at[0, 0], bc_r.at[b, l])
            tot = b_keep[xx, l] + b_core[xx, l].astype(F32)

            @pl.when(b == 0)
            def _():
                b0_acc[l] = tot
                b0_send[l] = tot.astype(BF16)
                for i in range(4):
                    j = lax.rem(i * 2 + l + 8 - y, 8)

                    @pl.when(j != 0)
                    def _():
                        go(rcopy(b0_send.at[l, pl.ds(80 * i, 80)], b0_recv.at[j], b0_s, b0_r,
                                 dev(x, i * 2 + l, z, c)))

            @pl.when(b == 1)
            def _():
                b1_acc[0:320] = tot
                by_z(b1_acc, b1_p32.at[l])
                b1_p16[l] = b1_p32[l].astype(BF16)
                for j in range(1, NZ):
                    go(rcopy(b1_p16.at[l, zo(j)], b1_recv.at[j, l], b1_s, b1_r, dev(x, y, zo(j), c)))

            wb = jnp.concatenate(
                [jnp.where(lane_lo[0:160], wu[q, 0:160, 128:256], wu[q, 480:640, 128:256]),
                 jnp.where(lane_lo[0:160], wu[q, 160:320, 128:256], wu[q, 320:480, 128:256])],
                axis=0).astype(F32)
            t = row_sums(halves, tot * wb)
            g_loc[pl.ds(q, 1), :] += t[0:1]
            g_loc[pl.ds(8 + q, 1), :] += t[1:2]

    a_acc[:, 320:336] = jnp.zeros((2, 16, 128), F32)
    b1_acc[320:336] = jnp.zeros((16, 128), F32)
    a1_p32[:, 40:48] = jnp.zeros((8, 8, 128), F32)
    b1_p32[:, :, 40:48] = jnp.zeros((2, 8, 8, 128), F32)
    bx_send[:, 80:96] = jnp.zeros((2, 16, 128), F32)
    a_fin0[80:96] = jnp.zeros((16, 128), F32)
    b_fin[96:112] = jnp.zeros((16, 128), F32)

    before = None
    for l in range(2):
        for k in (2, 1, 3, 0):
            chunk(l, k)
            if before:
                chip_sum(*before)
            before = (l, k)
    x_relay(0)
    chip_sum(*before)

    grow = pl.multiple_of(c * 8, 8)
    gorow = pl.multiple_of(oc * 8, 8)
    go(rcopy(g_loc.at[pl.ds(gorow, 8)], g_core, gc_s, gc_r, part_dev))
    x_relay(1)

    def spread(buf, own, ss, rs, count, to):
        for k in range(1, count):
            go(rcopy(buf.at[own], buf.at[own], ss, rs, to(k)))

    def sum8(v):
        return ((v[0] + v[1]) + (v[2] + v[3])) + ((v[4] + v[5]) + (v[6] + v[7]))

    got(g_core, gc_r)
    g_z[z] = g_loc[pl.ds(grow, 8)] + g_core[...]
    spread(g_z, z, gz_s, gz_r, NZ, lambda k: dev(x, y, zo(k), c))

    def x_done(l):
        got(ax_recv.at[l, pl.ds(0, 4)], ax_r.at[l])
        for i, (m, n) in enumerate(((4, 2), (1, 5))):
            a_acc[l, 160 * i:160 * i + 160] += ax_recv[l, m].astype(F32) + ax_recv[l, n].astype(F32)

    x_done(0)
    ay_send[...] = a_acc[0, 0:320].astype(BF16)
    for i in range(4):
        j = lax.rem(i * 2 + 8 - y, 8)

        @pl.when(j != 0)
        def _():
            go(rcopy(ay_send.at[pl.ds(80 * i, 80)], ay_recv.at[j], ay_s, ay_r, dev(x, i * 2, z, c)))

    x_done(1)
    by_z(a_acc.at[1], a1_p32)
    a1_p16[...] = a1_p32[...].astype(BF16)
    for j in range(1, NZ):
        go(rcopy(a1_p16.at[zo(j)], a1_recv.at[j], a1_s, a1_r, dev(x, y, zo(j), c)))

    got(b0_recv.at[pl.ds(1, 7)], b0_r)
    t = b0_acc[yl, pl.ds(pl.multiple_of(yh * 80, 16), 80)]
    for j in range(1, NY):
        t = t + b0_recv[j].astype(F32)
    bx_send[0, 0:80] = t
    got(b1_recv.at[pl.ds(1, 7)], b1_r)
    for l in range(2):
        t = b1_p32[l, z]
        for j in range(1, NZ):
            t = t + b1_recv[j, l].astype(F32)
        bx_send[1, 48 * l:48 * l + 48] = t
    for k in range(1, NX):
        xx = xo(k)

        @pl.when(lax.div(xx, 2) == c)
        def _():
            go(rcopy(bx_send.at[lax.rem(xx, 2)], bx_recv.at[k - 1], bx_s, bx_r, dev(xx, y, z, c)))

    got(g_z.at[pl.ds(0, 7)], gz_r)
    g_y[y] = sum8(g_z)
    spread(g_y, y, gy_s, gy_r, NY, lambda k: dev(x, yo(k), z, c))

    @pl.when(yl == 0)
    def _():
        got(ay_recv.at[pl.ds(1, 7)], ay_r)
        t = a_acc[0, pl.ds(pl.multiple_of(yh * 80, 16), 80)]
        for j in range(1, NY):
            t = t + ay_recv[j].astype(F32)
        a_fin0[0:80] = t
        for i in range(NZ):
            az0_send[i] = a_fin0[10 * i:10 * i + 16]
        az_recv[z] = az0_send[z]
        for k in range(1, NZ):
            go(rcopy(az0_send.at[zo(k)], az_recv.at[z], az_s, az_r, dev(x, y, zo(k), c)))

    got(a1_recv.at[pl.ds(1, 7)], a1_r)
    t = a1_p32[z]
    for j in range(1, NZ):
        t = t + a1_recv[j].astype(F32)
    a_fin1[...] = t
    for i in range(4):
        az1_send[i] = a_fin1[10 * i:10 * i + 16]
    for i in range(4):
        @pl.when(y != 2 * i + 1)
        def _():
            go(rcopy(az1_send.at[i], az_recv.at[y], az_s, az_r, dev(x, 2 * i + 1, z, c)))

        @pl.when(y == 2 * i + 1)
        def _():
            az_recv[y] = az1_send[i]

    slot = jnp.where(odd == 1, y, z)

    @pl.when(mine)
    def _():
        got(bx_recv, bx_r)
        b_fin[0:96] = (bx_send[odd] + bx_recv[0]) + (bx_recv[1] + bx_recv[2])

        @pl.when(odd == 0)
        def _():
            for n in range(8):
                bz_send[n] = b_fin[10 * n:10 * n + 16]

        @pl.when(odd == 1)
        def _():
            for n in range(8):
                o = (n % 2) * 48 + (n // 2) * 10
                bz_send[n] = b_fin[o:o + 16]

        bz_recv[slot] = bz_send[slot]
        for k in range(8):
            n = lax.rem(slot + k, 8)
            to_y = jnp.where(odd == 1, n, y)
            to_z = jnp.where(odd == 1, z, n)
            for o in range(0 if k else 1, 2):
                go(rcopy(bz_send.at[n], bz_recv.at[slot], bz_s, bz_r, dev(x, to_y, to_z, oc if o else c)))

    got(g_y.at[pl.ds(0, 7)], gy_r)
    g_x[x] = sum8(g_y)
    spread(g_x, x, gx_s, gx_r, NX, lambda k: dev(xo(k), y, z, c))

    got(az_recv.at[pl.ds(0, 7)], az_r)
    wg_out[:, 0:128] = sum8(az_recv)[0:10]

    @pl.when(mine)
    def _():
        got(bz_recv.at[pl.ds(0, 7)], bz_r)

    @pl.when(jnp.logical_not(mine))
    def _():
        got(bz_recv, bz_r)

    tb = sum8(bz_recv)
    tb = jnp.where(c == 0, tb, pltpu.roll(tb, 64, 1))
    wg_out[:, 128:192] = tb[0:10, 0:64]

    got(g_x.at[pl.ds(0, 3)], gx_r)
    g_mine[...] = (g_x[0] + g_x[1]) + (g_x[2] + g_x[3])
    gf = go(rcopy(g_mine, g_full, gf_s, gf_r, part_dev))
    gf.wait_recv()
    gg_out[pl.ds(grow, 8)] = g_mine[...]
    gg_out[pl.ds(gorow, 8)] = g_full[...]

    gf.wait_send()
    sent(wp.at[pl.ds(0, 3)], wx_s)
    sent(wp.at[pl.ds(0, 4)], wy_s)
    sent(wp.at[pl.ds(0, 8)], wc_s)
    sent(a_send, ac_s)
    sent(b_send.at[pl.ds(0, 2)], bc_s)
    sent(ax_send, ax_s)
    sent(g_core, gc_s)
    sent(g_z.at[pl.ds(0, 7)], gz_s)
    sent(g_y.at[pl.ds(0, 7)], gy_s)
    sent(g_x.at[pl.ds(0, 3)], gx_s)
    sent(b0_recv.at[pl.ds(1, 7)], b0_s)
    sent(b1_recv.at[pl.ds(1, 7)], b1_s)
    sent(a1_recv.at[pl.ds(1, 7)], a1_s)

    @pl.when(yl == 0)
    def _():
        sent(ay_recv.at[pl.ds(0, 3)], ay_s)
        sent(az_recv.at[pl.ds(0, 7)], az_s)
        sent(az_recv.at[pl.ds(0, 4)], az_s)

    @pl.when(yl == 1)
    def _():
        sent(ay_recv.at[pl.ds(0, 4)], ay_s)
        sent(az_recv.at[pl.ds(0, 3)], az_s)

    @pl.when(mine)
    def _():
        sent(bx_recv.at[0], bx_s)
        sent(bz_recv, bz_s)
        sent(bz_recv.at[pl.ds(0, 7)], bz_s)

    @pl.when(jnp.logical_not(mine))
    def _():
        sent(bx_recv.at[pl.ds(0, 2)], bx_s)


def leave(wg_in, gg_in, gain, wg_out, gg_out):
    wg_out[...] = wg_in[...]
    both = jnp.concatenate([gg_in[0:8], gg_in[8:16]], axis=1)
    for q in range(8):
        for i in range(5):
            r = q * 5 + i
            gg_out[r:r + 1] = both[q:q + 1, 128 * i:128 * i + 128] / gain[r:r + 1]


def on_device(hidden, targets, head_weight, norm_gain):
    dma = pltpu.SemaphoreType.DMA
    vm = pltpu.VMEM
    scratch = [
        vm((TOK,), jnp.int32), vm((192, 320), BF16), vm((1, D), F32),
        vm((TOK, D), BF16), vm((TOK, D), BF16),
        vm((16, 480, 128), BF16), vm((8, QW, 256), BF16), vm((TOK, 256), F32), vm((TOK, 256), BF16),
        vm((4, 2, 320, 128), F32), vm((4, 2, 320, 128), BF16), vm((4, 2, 320, 128), BF16),
        vm((4, 2, 320, 128), F32), vm((4, 2, 320, 128), BF16), vm((4, 2, 320, 128), BF16),
        vm((2, 6, 160, 128), BF16), vm((2, 6, 160, 128), BF16), vm((2, 2, 160, 128), F32),
        vm((2, 336, 128), F32),
        vm((320, 128), BF16), vm((8, 80, 128), BF16),
        vm((8, 48, 128), F32), vm((8, 48, 128), BF16), vm((8, 48, 128), BF16),
        vm((96, 128), F32), vm((48, 128), F32),
        vm((8, 16, 128), F32), vm((4, 16, 128), F32), vm((8, 16, 128), F32),
        vm((2, 320, 128), BF16), vm((2, 320, 128), F32), vm((8, 80, 128), BF16),
        vm((336, 128), F32), vm((2, 8, 48, 128), F32), vm((2, 8, 48, 128), BF16), vm((8, 2, 48, 128), BF16),
        vm((2, 96, 128), F32), vm((3, 96, 128), F32),
        vm((112, 128), F32), vm((8, 16, 128), F32), vm((8, 16, 128), F32),
        vm((16, 320), F32), vm((8, 320), F32), vm((4, 8, 320), F32),
        vm((8, 8, 320), F32), vm((8, 8, 320), F32), vm((8, 320), F32), vm((8, 320), F32),
        dma((7,)),
        dma, dma((3, 2)), dma, dma((4,)), dma, dma((4, 2)), dma, dma((4, 2)), dma, dma((2, 2)),
        dma, dma((2, 2)), dma((2,)), dma, dma, dma, dma, dma, dma,
        dma, dma, dma, dma, dma, dma, dma, dma,
        dma, dma, dma, dma, dma, dma, dma, dma, dma, dma,
    ]
    vspec = pl.BlockSpec(memory_space=pltpu.VMEM)
    wg, gg = pl.pallas_call(
        kernel,
        out_shape=(jax.ShapeDtypeStruct((10, V), F32), jax.ShapeDtypeStruct((16, 320), F32)),
        in_specs=[pl.BlockSpec(memory_space=pl.ANY)] * 4,
        out_specs=(vspec, vspec),
        scratch_shapes=scratch,
        compiler_params=pltpu.CompilerParams(
            collective_id=0, has_side_effects=True, vmem_limit_bytes=56 * 1024 * 1024),
        cost_estimate=pl.CostEstimate(flops=3 * 2 * TOK * D * V, bytes_accessed=TOK * D * 2,
                                      transcendentals=TOK * V),
    )(hidden, targets, head_weight.T, norm_gain.reshape(1, D))
    wg, gg = pl.pallas_call(
        leave,
        out_shape=(jax.ShapeDtypeStruct((10, V), F32), jax.ShapeDtypeStruct((40, 128), F32)),
        in_specs=[vspec] * 3,
        out_specs=(vspec, vspec),
    )(wg, gg, norm_gain.reshape(40, 128))
    return wg, gg.reshape(D)


def solution(mesh):
    placed = (P(("section", "dp"), None), P(("section", "dp")), P("section", None), P())
    return jax.shard_map(
        on_device,
        mesh=mesh,
        in_specs=placed,
        out_specs=(P(("section", "dp"), None), P()),
        check_vma=False,
    )
```

```python
import jax
import jax.numpy as jnp
from jax import lax
from jax.experimental import pallas as pl
from jax.experimental.pallas import tpu as pltpu
from jax.sharding import PartitionSpec as P

D = 5120
V = 192
TOK = 384
NX, NY, NZ = 4, 8, 8
QW = 640
MESH = pl.DeviceIdType.MESH
F32 = jnp.float32
BF16 = jnp.bfloat16
SCALE = 1.0 / TOK**0.5


def kernel(
    hid, tgt_in, wt_in, gain_in, wg_out, gg_out,
    tgt, wt, gain, h, s, wp, wu, logit, dle,
    terms, a_send, a_core, a_tot, b_send, b_core, b_tot,
    ax_send, ax_recv, a_pend, a_acc,
    ay_send, ay_recv, a1_p32, a1_p16, a1_recv, a_fin0, a_fin1, az0_send, az1_send, az_recv,
    b0_send, b0_recv, b1_p32, b1_p16, b1_recv,
    bx_own, bx_send, bx_recv, b_fin, bz_send, bz_recv,
    g_loc, g_core, g_x, g_y, g_z,
    hsem,
    wx_s, wx_r, wy_s, wy_r, wc_s, wc_r, ac_s, ac_r, bc_s, bc_r,
    ax_s, axr_r, ax_r, ay_s, ay_r, a1_s, a1_r, az_s, az_r,
    b0_s, b0_r, b1_s, b1_r, bx_s, bx_r, bz_s, bz_r,
    gc_s, gc_r, gx_s, gx_r, gy_s, gy_r, gz_s, gz_r,
):
    sec = lax.axis_index("section")
    dp = lax.axis_index("dp")
    c = lax.rem(sec, 2)
    yl = lax.rem(lax.div(sec, 2), 2)
    x = lax.div(sec, 4)
    yh = lax.div(dp, NZ)
    z = lax.rem(dp, NZ)
    y = yh * 2 + yl
    oc = 1 - c
    odd = lax.rem(x, 2)
    mine = lax.div(x, 2) == c

    def dev(x_, y_, z_, c_):
        return (x_ * 4 + lax.rem(y_, 2) * 2 + c_, lax.div(y_, 2) * NZ + z_)

    def xo(k):
        return lax.rem(x + k, NX)

    def yo(k):
        return lax.rem(y + k, NY)

    def zo(k):
        return lax.rem(z + k, NZ)

    def rcopy(src, dst, ss, rs, to):
        return pltpu.make_async_remote_copy(
            src_ref=src, dst_ref=dst, send_sem=ss, recv_sem=rs,
            device_id=to, device_id_type=MESH)

    barrier = pltpu.get_barrier_semaphore()
    peers = [dev(x, y, z, oc)]
    peers += [dev(xo(k), y, z, c) for k in range(1, NX)]
    peers += [dev(x, yo(k), z, c) for k in range(1, NY)]
    peers += [dev(x, y, zo(k), c) for k in range(1, NZ)]
    for p in peers:
        pl.semaphore_signal(barrier, inc=1, device_id=p, device_id_type=MESH)

    def fetch(src, dst, i):
        cp = pltpu.make_async_copy(src, dst, hsem.at[i])
        cp.start()
        return cp

    wcopy = fetch(wt_in, wt, 4)
    hcopies = [fetch(hid.at[pl.ds(96 * i, 96)], h.at[pl.ds(96 * i, 96)], i) for i in range(4)]
    gcopy = fetch(gain_in, gain, 5)
    tcopy = fetch(tgt_in, tgt, 6)

    eye = (lax.broadcasted_iota(jnp.int32, (320, 320), 0)
           == lax.broadcasted_iota(jnp.int32, (320, 320), 1)).astype(BF16)
    wcopy.wait()
    w = lax.dot_general(eye, wt[...], (((1,), (1,)), ((), ())), preferred_element_type=F32)
    wp[sec, 0:320, :] = w[:, 0:128].astype(BF16)
    wp[sec, 320:480, :] = jnp.concatenate(
        [w[0:160, 128:192], w[160:320, 128:192]], axis=1).astype(BF16)

    pl.semaphore_wait(barrier, len(peers))

    def go(cp):
        cp.start()
        return cp

    def got(ref, rs):
        rcopy(ref, ref, wx_s, rs, dev(x, y, z, oc)).wait_recv()

    def sent(ref, ss):
        rcopy(ref, ref, ss, gc_r, dev(x, y, z, oc)).wait_send()

    def shard(k, l, cc):
        return xo(NX - k if k else 0) * 4 + l * 2 + cc

    def piece(sh, i):
        return wp.at[sh, pl.ds((0, 128, 240, 368)[i], (128, 112)[i % 2])]

    wx, wc = {}, {}

    def send_x(k, i):
        wx[(k, i)] = go(rcopy(piece(sec, i), piece(sec, i), wx_s, wx_r.at[k - 1, i],
                              dev(xo(k), y, z, c)))

    def fwd_y(k, i):
        sh = shard(k, yl, c)
        go(rcopy(piece(sh, i), piece(sh, i), wy_s, wy_r.at[k], dev(x, yo(1 if i < 2 else NY - 1), z, c)))

    def fwd_c(k, j):
        sh = shard(k, yl if j == 0 else 1 - yl, c)
        wc[(k, j)] = go(rcopy(wp.at[sh], wp.at[sh], wc_s, wc_r.at[k, j], dev(x, y, z, oc)))

    for i in range(4):
        send_x(1, i)
        send_x(3, (i + 2) % 4)
        fwd_y(0, (i // 2) + 2 * (i % 2))
    fwd_c(0, 0)

    def rows(i, carry):
        r0 = pl.multiple_of(i * 16, 16)
        acc = jnp.zeros((16, 128), F32)
        for j in range(D // 128):
            v = h[pl.ds(r0, 16), j * 128:(j + 1) * 128].astype(F32)
            acc = acc + v * v
        ms = jnp.sum(acc, axis=1, keepdims=True) * (1.0 / D)
        r = jnp.broadcast_to(lax.rsqrt(ms + 1e-05), (16, 128))
        for j in range(D // 128):
            v = h[pl.ds(r0, 16), j * 128:(j + 1) * 128].astype(F32)
            gj = gain[:, j * 128:(j + 1) * 128]
            s[pl.ds(r0, 16), j * 128:(j + 1) * 128] = ((v * r) * gj).astype(BF16)
        return carry

    def block(i):
        if i == 0:
            gcopy.wait()
        if i % 2 == 0:
            hcopies[i // 2].wait()
        lax.fori_loop(3 * i, 3 * i + 3, rows, 0)

    def take_x(k, i):
        wx[(k, i)].wait_recv()
        if k == (1 if i < 2 else 3):
            sh = shard(k, yl, c)
            wx[(2, i)] = go(rcopy(piece(sh, i), piece(sh, i), wx_s, wx_r.at[1, i],
                                  dev(xo(k), y, z, c)))
        fwd_y(k, i)

    def take_y(k):
        got(wp.at[0], wy_r.at[k])
        fwd_c(k, 1)

    def unpack(k, j):
        l = yl if j == 0 else 1 - yl
        q = xo(NX - k if k else 0) * 2 + l
        for cc in range(2):
            sh = q * 2 + cc
            wu[q, cc * 320:(cc + 1) * 320, 0:128] = wp[sh, 0:320, :]
            b = wp[sh, 320:480, :]
            wu[q, cc * 320:cc * 320 + 160, 128:256] = b
            wu[q, cc * 320 + 160:(cc + 1) * 320, 128:256] = pltpu.roll(
                b.astype(F32), 64, 1).astype(BF16)
        return q

    def add_logits(k, j):
        wc[(k, j)].wait_recv()
        q = unpack(k, j)
        part = jnp.dot(s[:, pl.ds(pl.multiple_of(q * QW, 128), QW)], wu[q],
                       preferred_element_type=F32)
        if (k, j) == (0, 0):
            logit[...] = part
        else:
            logit[...] += part

    for i in range(5):
        block(i)
    for i in range(4):
        take_x(1, i)
        take_x(3, (i + 2) % 4)
        if i < 3:
            block(5 + i)
    fwd_c(1, 0)
    fwd_c(3, 0)
    take_y(0)
    add_logits(0, 0)
    take_x(2, 0)
    take_x(2, 2)
    add_logits(1, 0)
    take_x(2, 1)
    take_x(2, 3)
    fwd_c(2, 0)
    add_logits(3, 0)
    add_logits(0, 1)
    add_logits(2, 0)
    take_y(1)
    take_y(3)
    add_logits(1, 1)
    take_y(2)
    add_logits(3, 1)
    add_logits(2, 1)

    lane = lax.broadcasted_iota(jnp.int32, (TOK, 256), 1)
    tcopy.wait()
    t_col = jnp.transpose(jnp.broadcast_to(tgt[...].reshape(1, TOK).astype(F32), (128, TOK)))
    tc = jnp.concatenate([t_col, t_col], axis=1)
    onehot = (tc == lane.astype(F32)).astype(F32)
    lg = jnp.where(lane < V, logit[...], -3e38)
    m = jnp.max(lg, axis=1, keepdims=True)
    e = jnp.where(lane < V, jnp.exp(lg - m), 0.0)
    p = e / jnp.sum(e, axis=1, keepdims=True)
    dl = ((p - onehot) * SCALE).astype(BF16)
    up = dl[:, 128:256].astype(F32)
    dle[:, 0:128] = dl[:, 0:128]
    dle[:, 128:256] = (up + pltpu.roll(up, 64, 1)).astype(BF16)

    lane_lo = lax.broadcasted_iota(jnp.int32, (320, 128), 1) < 64
    pick_row = lax.broadcasted_iota(jnp.int32, (8, 128), 0)
    pick_half = (lax.broadcasted_iota(jnp.int32, (8, 128), 1) >= 64).astype(jnp.int32)
    ones = jnp.ones((8, 128), BF16)
    halves = (pick_row == pick_half).astype(BF16)
    part_dev = dev(x, y, z, oc)
    g_loc[...] = jnp.zeros((16, 320), F32)

    def packed(n):
        return jnp.where(lane_lo, terms[n, 0:320, 128:256], terms[n, 320:640, 128:256])

    def x_go(l, n):
        rs = axr_r.at[l, n // 3] if n % 3 == 0 else ax_r.at[l]
        go(rcopy(ax_send.at[l, n], ax_recv.at[l, n], ax_s, rs, dev(xo(1 if n < 3 else 3), y, z, c)))

    def x_relay(l):
        for i in range(2):
            got(ax_recv.at[l, 3 * i], axr_r.at[l, i])
            ax_send[l, 3 * i + 2] = (a_pend[l, i] + ax_recv[l, 3 * i].astype(F32)).astype(BF16)
            x_go(l, 3 * i + 2)

    def row_sums(pick, v):
        hi = v.astype(BF16)
        lo = (v - hi.astype(F32)).astype(BF16)
        dims = (((1,), (1,)), ((), ()))
        return (lax.dot_general(pick, hi, dims, preferred_element_type=F32)
                + lax.dot_general(pick, lo, dims, preferred_element_type=F32))

    def by_z(src, dst):
        for j in range(NZ):
            for i in range(4):
                dst[j, 10 * i:10 * i + 16] = src[80 * i + 10 * j:80 * i + 10 * j + 16]

    def gain_a(n):
        l, k = todo[n]
        q = xo(k) * 2 + l
        wa = wu[q, pl.ds(pl.multiple_of(c * 320, 16), 320), 0:128].astype(F32)
        row = c * 8 + q
        g_loc[pl.ds(row, 1), :] += row_sums(ones, a_tot[n] * wa)[0:1]

    def gain_b(l, b):
        q = (c * 2 + b) * 2 + l
        wb = jnp.concatenate(
            [jnp.where(lane_lo[0:160], wu[q, 0:160, 128:256], wu[q, 480:640, 128:256]),
             jnp.where(lane_lo[0:160], wu[q, 160:320, 128:256], wu[q, 320:480, 128:256])],
            axis=0).astype(F32)
        t = row_sums(halves, b_tot[l * 4 + place(b), 0:320] * wb)
        g_loc[pl.ds(q, 1), :] += t[0:1]
        g_loc[pl.ds(8 + q, 1), :] += t[1:2]

    todo = [(l, k) for l in range(2) for k in (2, 1, 3, 0)]

    def place(b):
        k = lax.rem(c * 2 + b + NX - x, NX)
        return jnp.where(k == 0, 3, jnp.where(k == 3, 2, jnp.where(k == 2, 0, 1)))

    def step(n):
        r, m = n - 1, n - 3
        if 0 <= m:
            l, k = todo[m]
            xx = xo(k)
            own = lax.div(xx, 2) == c
            b = lax.rem(xx, 2)
            got(a_core.at[0], ac_r.at[m])

            @pl.when(own)
            def _():
                got(b_core.at[0], bc_r.at[m])

        if n < 8:
            q = xo(todo[n][1]) * 2 + todo[n][0]
            terms[n] = lax.dot_general(
                s[:, pl.ds(pl.multiple_of(q * QW, 128), QW)], dle[...],
                (((0,), (0,)), ((), ())), preferred_element_type=F32)
        if 0 <= r < 8:
            a_send[r] = terms[r, pl.ds(pl.multiple_of(oc * 320, 16), 320), 0:128].astype(BF16)
            b_send[r] = packed(r).astype(BF16)
        if 0 <= m:
            tot = (terms[m, pl.ds(pl.multiple_of(c * 320, 16), 320), 0:128]
                   + a_core[m].astype(F32))
            a_tot[m] = tot
            if k == 0:
                a_acc[l, 0:320] = tot
            if k == 1:
                ax_send[l, 1] = tot[160:320].astype(BF16)
                a_pend[l, 0] = tot[0:160]
            if k == 2:
                ax_send[l, 0] = tot[0:160].astype(BF16)
                ax_send[l, 3] = tot[160:320].astype(BF16)
            if k == 3:
                ax_send[l, 4] = tot[0:160].astype(BF16)
                a_pend[l, 1] = tot[160:320]
            tot = packed(m) + b_core[m].astype(F32)
            b_tot[m, 0:320] = tot
            b0_send[m] = tot.astype(BF16)
        if 0 <= r < 8:
            go(rcopy(a_send.at[r], a_core.at[r], ac_s, ac_r.at[r], part_dev))

            @pl.when(lax.div(xo(todo[r][1]), 2) != c)
            def _():
                go(rcopy(b_send.at[r], b_core.at[r], bc_s, bc_r.at[r], part_dev))

        if 0 <= m:
            for i in {0: (), 1: (1,), 2: (0, 3), 3: (4,)}[k]:
                x_go(l, i)

            @pl.when(jnp.logical_and(own, b == 0))
            def _():
                for i in range(4):
                    j = lax.rem(i * 2 + l + 8 - y, 8)

                    @pl.when(j != 0)
                    def _():
                        go(rcopy(b0_send.at[m, pl.ds(80 * i, 80)], b0_recv.at[j], b0_s, b0_r,
                                 dev(x, i * 2 + l, z, c)))

            @pl.when(jnp.logical_and(own, b == 1))
            def _():
                by_z(b_tot.at[m], b1_p32.at[l])
                b1_p16[l] = b1_p32[l].astype(BF16)
                for j in range(1, NZ):
                    go(rcopy(b1_p16.at[l, zo(j)], b1_recv.at[j, l], b1_s, b1_r, dev(x, y, zo(j), c)))

    a_acc[:, 320:336] = jnp.zeros((2, 16, 128), F32)
    b_tot[:, 320:336] = jnp.zeros((8, 16, 128), F32)
    a1_p32[:, 40:48] = jnp.zeros((8, 8, 128), F32)
    b1_p32[:, :, 40:48] = jnp.zeros((2, 8, 8, 128), F32)
    bx_own[:, 80:96] = jnp.zeros((2, 16, 128), F32)
    a_fin0[80:96] = jnp.zeros((16, 128), F32)
    b_fin[96:112] = jnp.zeros((16, 128), F32)

    for n in range(11):
        step(n)
        if n >= 8:
            gain_a(n - 8)
    x_relay(0)
    for n in range(3, 8):
        gain_a(n)
        if n == 5:
            x_relay(1)
    for l in range(2):
        for b in range(2):
            gain_b(l, b)

    grow = pl.multiple_of(c * 8, 8)
    gorow = pl.multiple_of(oc * 8, 8)
    go(rcopy(g_loc.at[pl.ds(gorow, 8)], g_core, gc_s, gc_r, part_dev))

    def spread(buf, own, ss, rs, count, to):
        for k in range(1, count):
            go(rcopy(buf.at[own], buf.at[own], ss, rs, to(k)))

    def sum8(v):
        return ((v[0] + v[1]) + (v[2] + v[3])) + ((v[4] + v[5]) + (v[6] + v[7]))

    got(g_core, gc_r)
    g_z[z] = g_loc[pl.ds(grow, 8)] + g_core[...]
    spread(g_z, z, gz_s, gz_r, NZ, lambda k: dev(x, y, zo(k), c))

    def x_done(l):
        got(ax_recv.at[l, pl.ds(0, 4)], ax_r.at[l])
        for i, (m, n) in enumerate(((4, 2), (1, 5))):
            a_acc[l, 160 * i:160 * i + 160] += ax_recv[l, m].astype(F32) + ax_recv[l, n].astype(F32)

    x_done(0)
    ay_send[...] = a_acc[0, 0:320].astype(BF16)
    for i in range(4):
        j = lax.rem(i * 2 + 8 - y, 8)

        @pl.when(j != 0)
        def _():
            go(rcopy(ay_send.at[pl.ds(80 * i, 80)], ay_recv.at[j], ay_s, ay_r, dev(x, i * 2, z, c)))

    x_done(1)
    by_z(a_acc.at[1], a1_p32)
    a1_p16[...] = a1_p32[...].astype(BF16)
    for j in range(1, NZ):
        go(rcopy(a1_p16.at[zo(j)], a1_recv.at[j], a1_s, a1_r, dev(x, y, zo(j), c)))

    got(b0_recv.at[pl.ds(1, 7)], b0_r)
    t = b_tot[yl * 4 + place(0), pl.ds(pl.multiple_of(yh * 80, 16), 80)]
    for j in range(1, NY):
        t = t + b0_recv[j].astype(F32)
    bx_own[0, 0:80] = t
    got(b1_recv.at[pl.ds(1, 7)], b1_r)
    for l in range(2):
        t = b1_p32[l, z]
        for j in range(1, NZ):
            t = t + b1_recv[j, l].astype(F32)
        bx_own[1, 48 * l:48 * l + 48] = t
    bx_send[...] = bx_own[...].astype(BF16)
    for k in range(1, NX):
        xx = xo(k)

        @pl.when(lax.div(xx, 2) == c)
        def _():
            go(rcopy(bx_send.at[lax.rem(xx, 2)], bx_recv.at[k - 1], bx_s, bx_r, dev(xx, y, z, c)))

    got(g_z.at[pl.ds(0, 7)], gz_r)
    g_y[y] = sum8(g_z)
    spread(g_y, y, gy_s, gy_r, NY, lambda k: dev(x, yo(k), z, c))

    @pl.when(yl == 0)
    def _():
        got(ay_recv.at[pl.ds(1, 7)], ay_r)
        t = a_acc[0, pl.ds(pl.multiple_of(yh * 80, 16), 80)]
        for j in range(1, NY):
            t = t + ay_recv[j].astype(F32)
        a_fin0[0:80] = t
        for i in range(NZ):
            az0_send[i] = a_fin0[10 * i:10 * i + 16]
        az_recv[z] = az0_send[z]
        for k in range(1, NZ):
            go(rcopy(az0_send.at[zo(k)], az_recv.at[z], az_s, az_r, dev(x, y, zo(k), c)))

    got(a1_recv.at[pl.ds(1, 7)], a1_r)
    t = a1_p32[z]
    for j in range(1, NZ):
        t = t + a1_recv[j].astype(F32)
    a_fin1[...] = t
    for i in range(4):
        az1_send[i] = a_fin1[10 * i:10 * i + 16]
    for i in range(4):
        @pl.when(y != 2 * i + 1)
        def _():
            go(rcopy(az1_send.at[i], az_recv.at[y], az_s, az_r, dev(x, 2 * i + 1, z, c)))

        @pl.when(y == 2 * i + 1)
        def _():
            az_recv[y] = az1_send[i]

    slot = jnp.where(odd == 1, y, z)

    @pl.when(mine)
    def _():
        got(bx_recv, bx_r)
        v = bx_recv[...].astype(F32)
        b_fin[0:96] = (bx_own[odd] + v[0]) + (v[1] + v[2])

        @pl.when(odd == 0)
        def _():
            for n in range(8):
                bz_send[n] = b_fin[10 * n:10 * n + 16]

        @pl.when(odd == 1)
        def _():
            for n in range(8):
                o = (n % 2) * 48 + (n // 2) * 10
                bz_send[n] = b_fin[o:o + 16]

        bz_recv[slot] = bz_send[slot]
        for k in range(8):
            n = lax.rem(slot + k, 8)
            to_y = jnp.where(odd == 1, n, y)
            to_z = jnp.where(odd == 1, z, n)
            for o in range(0 if k else 1, 2):
                go(rcopy(bz_send.at[n], bz_recv.at[slot], bz_s, bz_r, dev(x, to_y, to_z, oc if o else c)))

    got(g_y.at[pl.ds(0, 7)], gy_r)
    g_x[c, x] = sum8(g_y)
    mine_x = g_x.at[c, x]
    for k in range(1, NX):
        go(rcopy(mine_x, mine_x, gx_s, gx_r, dev(xo(k), y, z, c)))
    for k in range(NX):
        go(rcopy(mine_x, mine_x, gx_s, gx_r, dev(xo(k), y, z, oc)))

    got(az_recv.at[pl.ds(0, 7)], az_r)
    wg_out[:, 0:128] = sum8(az_recv)[0:10]

    @pl.when(mine)
    def _():
        got(bz_recv.at[pl.ds(0, 7)], bz_r)

    @pl.when(jnp.logical_not(mine))
    def _():
        got(bz_recv, bz_r)

    tb = sum8(bz_recv)
    tb = jnp.where(c == 0, tb, pltpu.roll(tb, 64, 1))
    wg_out[:, 128:192] = tb[0:10, 0:64]

    got(g_z.at[pl.ds(0, 7)], gx_r)
    for i in range(2):
        gg_out[8 * i:8 * i + 8] = (g_x[i, 0] + g_x[i, 1]) + (g_x[i, 2] + g_x[i, 3])

    sent(wp.at[pl.ds(0, 3)], wx_s)
    sent(wp.at[pl.ds(0, 4)], wy_s)
    sent(wp.at[pl.ds(0, 8)], wc_s)
    sent(a_send, ac_s)
    sent(b_send.at[pl.ds(0, 4)], bc_s)
    sent(ax_send, ax_s)
    sent(g_core, gc_s)
    sent(g_z.at[pl.ds(0, 7)], gz_s)
    sent(g_y.at[pl.ds(0, 7)], gy_s)
    sent(g_z.at[pl.ds(0, 7)], gx_s)
    sent(b0_recv.at[pl.ds(1, 7)], b0_s)
    sent(b1_recv.at[pl.ds(1, 7)], b1_s)
    sent(a1_recv.at[pl.ds(1, 7)], a1_s)

    @pl.when(yl == 0)
    def _():
        sent(ay_recv.at[pl.ds(0, 3)], ay_s)
        sent(az_recv.at[pl.ds(0, 7)], az_s)
        sent(az_recv.at[pl.ds(0, 4)], az_s)

    @pl.when(yl == 1)
    def _():
        sent(ay_recv.at[pl.ds(0, 4)], ay_s)
        sent(az_recv.at[pl.ds(0, 3)], az_s)

    @pl.when(mine)
    def _():
        sent(bx_recv.at[0], bx_s)
        sent(bz_recv, bz_s)
        sent(bz_recv.at[pl.ds(0, 7)], bz_s)

    @pl.when(jnp.logical_not(mine))
    def _():
        sent(bx_recv.at[pl.ds(0, 2)], bx_s)


def leave(wg_in, gg_in, gain, wg_out, gg_out):
    wg_out[...] = wg_in[...]
    both = jnp.concatenate([gg_in[0:8], gg_in[8:16]], axis=1)
    for q in range(8):
        for i in range(5):
            r = q * 5 + i
            gg_out[r:r + 1] = both[q:q + 1, 128 * i:128 * i + 128] / gain[r:r + 1]


def on_device(hidden, targets, head_weight, norm_gain):
    dma = pltpu.SemaphoreType.DMA
    vm = pltpu.VMEM
    scratch = [
        vm((TOK,), jnp.int32), vm((192, 320), BF16), vm((1, D), F32),
        vm((TOK, D), BF16), vm((TOK, D), BF16),
        vm((16, 480, 128), BF16), vm((8, QW, 256), BF16), vm((TOK, 256), F32), vm((TOK, 256), BF16),
        vm((8, QW, 256), F32), vm((8, 320, 128), BF16), vm((8, 320, 128), BF16),
        vm((8, 320, 128), F32), vm((8, 320, 128), BF16), vm((8, 320, 128), BF16),
        vm((8, 336, 128), F32),
        vm((2, 6, 160, 128), BF16), vm((2, 6, 160, 128), BF16), vm((2, 2, 160, 128), F32),
        vm((2, 336, 128), F32),
        vm((320, 128), BF16), vm((8, 80, 128), BF16),
        vm((8, 48, 128), F32), vm((8, 48, 128), BF16), vm((8, 48, 128), BF16),
        vm((96, 128), F32), vm((48, 128), F32),
        vm((8, 16, 128), F32), vm((4, 16, 128), F32), vm((8, 16, 128), F32),
        vm((8, 320, 128), BF16), vm((8, 80, 128), BF16),
        vm((2, 8, 48, 128), F32), vm((2, 8, 48, 128), BF16), vm((8, 2, 48, 128), BF16),
        vm((2, 96, 128), F32), vm((2, 96, 128), BF16), vm((3, 96, 128), BF16),
        vm((112, 128), F32), vm((8, 16, 128), F32), vm((8, 16, 128), F32),
        vm((16, 320), F32), vm((8, 320), F32), vm((2, 4, 8, 320), F32),
        vm((8, 8, 320), F32), vm((8, 8, 320), F32),
        dma((7,)),
        dma, dma((3, 4)), dma, dma((4,)), dma, dma((4, 2)), dma, dma((8,)), dma, dma((8,)),
        dma, dma((2, 2)), dma((2,)), dma, dma, dma, dma, dma, dma,
        dma, dma, dma, dma, dma, dma, dma, dma,
        dma, dma, dma, dma, dma, dma, dma, dma,
    ]
    vspec = pl.BlockSpec(memory_space=pltpu.VMEM)
    wg, gg = pl.pallas_call(
        kernel,
        out_shape=(jax.ShapeDtypeStruct((10, V), F32), jax.ShapeDtypeStruct((16, 320), F32)),
        in_specs=[pl.BlockSpec(memory_space=pl.ANY)] * 4,
        out_specs=(vspec, vspec),
        scratch_shapes=scratch,
        compiler_params=pltpu.CompilerParams(
            collective_id=0, has_side_effects=True, vmem_limit_bytes=56 * 1024 * 1024),
        cost_estimate=pl.CostEstimate(flops=3 * 2 * TOK * D * V, bytes_accessed=TOK * D * 2,
                                      transcendentals=TOK * V),
    )(hidden, targets, head_weight.T, norm_gain.reshape(1, D))
    wg, gg = pl.pallas_call(
        leave,
        out_shape=(jax.ShapeDtypeStruct((10, V), F32), jax.ShapeDtypeStruct((40, 128), F32)),
        in_specs=[vspec] * 3,
        out_specs=(vspec, vspec),
    )(wg, gg, norm_gain.reshape(40, 128))
    return wg, gg.reshape(D)


def solution(mesh):
    placed = (P(("section", "dp"), None), P(("section", "dp")), P("section", None), P())
    return jax.shard_map(
        on_device,
        mesh=mesh,
        in_specs=placed,
        out_specs=(P(("section", "dp"), None), P()),
        check_vma=False,
    )
```

```python
import jax
import jax.numpy as jnp
from jax import lax
from jax.experimental import pallas as pl
from jax.experimental.pallas import tpu as pltpu
from jax.sharding import PartitionSpec as P

D = 5120
V = 192
TOK = 384
NX, NY, NZ = 4, 8, 8
QW = 640
MESH = pl.DeviceIdType.MESH
F32 = jnp.float32
BF16 = jnp.bfloat16
SCALE = 1.0 / TOK**0.5


def kernel(
    hid, tgt_in, wt_in, gain_in, wg_out, gg_out,
    tgt, wt, gain, h, s, wp, wu, logit, dle,
    terms, a_send, a_core, a_tot, b_send, b_core, b_tot,
    ax_send, ax_recv, a_pend, a_acc,
    ay_send, ay_recv, a1_p32, a1_p16, a1_recv, a_fin0, a_fin1, az0_send, az1_send, az_recv,
    b0_send, b0_recv, b1_p32, b1_p16, b1_recv,
    bx_own, bx_send, bx_recv, b_fin, bz_send, bz_recv,
    g_loc, g_core, g_x, g_y, g_z,
    hsem,
    wx_s, wx_r, wy_s, wy_r, wc_s, wc_r, ac_s, ac_r, bc_s, bc_r,
    ax_s, axr_r, ax_r, ay_s, ay_r, a1_s, a1_r, az_s, az_r,
    b0_s, b0_r, b1_s, b1_r, bx_s, bx_r, bz_s, bz_r,
    gc_s, gc_r, gx_s, gx_r, gy_s, gy_r, gz_s, gz_r,
):
    sec = lax.axis_index("section")
    dp = lax.axis_index("dp")
    c = lax.rem(sec, 2)
    yl = lax.rem(lax.div(sec, 2), 2)
    x = lax.div(sec, 4)
    yh = lax.div(dp, NZ)
    z = lax.rem(dp, NZ)
    y = yh * 2 + yl
    oc = 1 - c
    odd = lax.rem(x, 2)
    mine = lax.div(x, 2) == c

    def dev(x_, y_, z_, c_):
        return (x_ * 4 + lax.rem(y_, 2) * 2 + c_, lax.div(y_, 2) * NZ + z_)

    def xo(k):
        return lax.rem(x + k, NX)

    def yo(k):
        return lax.rem(y + k, NY)

    def zo(k):
        return lax.rem(z + k, NZ)

    def rcopy(src, dst, ss, rs, to):
        return pltpu.make_async_remote_copy(
            src_ref=src, dst_ref=dst, send_sem=ss, recv_sem=rs,
            device_id=to, device_id_type=MESH)

    barrier = pltpu.get_barrier_semaphore()
    peers = [dev(x, y, z, oc)]
    peers += [dev(xo(k), y, z, c) for k in range(1, NX)]
    peers += [dev(x, yo(k), z, c) for k in range(1, NY)]
    peers += [dev(x, y, zo(k), c) for k in range(1, NZ)]
    for p in peers:
        pl.semaphore_signal(barrier, inc=1, device_id=p, device_id_type=MESH)

    def fetch(src, dst, i):
        cp = pltpu.make_async_copy(src, dst, hsem.at[i])
        cp.start()
        return cp

    wcopy = fetch(wt_in, wt, 4)
    hcopies = [fetch(hid.at[pl.ds(96 * i, 96)], h.at[pl.ds(96 * i, 96)], i) for i in range(4)]
    gcopy = fetch(gain_in, gain, 5)
    tcopy = fetch(tgt_in, tgt, 6)

    eye = (lax.broadcasted_iota(jnp.int32, (320, 320), 0)
           == lax.broadcasted_iota(jnp.int32, (320, 320), 1)).astype(BF16)
    wcopy.wait()
    w = lax.dot_general(eye, wt[...], (((1,), (1,)), ((), ())), preferred_element_type=F32)
    wp[sec, 0:320, :] = w[:, 0:128].astype(BF16)
    wp[sec, 320:480, :] = jnp.concatenate(
        [w[0:160, 128:192], w[160:320, 128:192]], axis=1).astype(BF16)

    pl.semaphore_wait(barrier, len(peers))

    def go(cp):
        cp.start()
        return cp

    def got(ref, rs):
        rcopy(ref, ref, wx_s, rs, dev(x, y, z, oc)).wait_recv()

    def sent(ref, ss):
        rcopy(ref, ref, ss, gc_r, dev(x, y, z, oc)).wait_send()

    def shard(k, l, cc):
        return xo(NX - k if k else 0) * 4 + l * 2 + cc

    def piece(sh, i):
        return wp.at[sh, pl.ds((0, 128, 240, 368)[i], (128, 112)[i % 2])]

    wx, wc = {}, {}

    def send_x(k, i):
        wx[(k, i)] = go(rcopy(piece(sec, i), piece(sec, i), wx_s, wx_r.at[k - 1, i],
                              dev(xo(k), y, z, c)))

    def fwd_y(k, i):
        sh = shard(k, yl, c)
        go(rcopy(piece(sh, i), piece(sh, i), wy_s, wy_r.at[k], dev(x, yo(1 if i < 2 else NY - 1), z, c)))

    def fwd_c(k, j):
        sh = shard(k, yl if j == 0 else 1 - yl, c)
        wc[(k, j)] = go(rcopy(wp.at[sh], wp.at[sh], wc_s, wc_r.at[k, j], dev(x, y, z, oc)))

    for i in range(4):
        send_x(1, i)
        send_x(3, (i + 2) % 4)
        fwd_y(0, (i // 2) + 2 * (i % 2))
    fwd_c(0, 0)

    def rows(i, carry):
        r0 = pl.multiple_of(i * 16, 16)
        acc = jnp.zeros((16, 128), F32)
        for j in range(D // 128):
            v = h[pl.ds(r0, 16), j * 128:(j + 1) * 128].astype(F32)
            acc = acc + v * v
        ms = jnp.sum(acc, axis=1, keepdims=True) * (1.0 / D)
        r = jnp.broadcast_to(lax.rsqrt(ms + 1e-05), (16, 128))
        for j in range(D // 128):
            v = h[pl.ds(r0, 16), j * 128:(j + 1) * 128].astype(F32)
            gj = gain[:, j * 128:(j + 1) * 128]
            s[pl.ds(r0, 16), j * 128:(j + 1) * 128] = ((v * r) * gj).astype(BF16)
        return carry

    def block(i):
        if i == 0:
            gcopy.wait()
        if i % 2 == 0:
            hcopies[i // 2].wait()
        lax.fori_loop(3 * i, 3 * i + 3, rows, 0)

    def take_x(k, i):
        wx[(k, i)].wait_recv()
        if k == (1 if i < 2 else 3):
            sh = shard(k, yl, c)
            wx[(2, i)] = go(rcopy(piece(sh, i), piece(sh, i), wx_s, wx_r.at[1, i],
                                  dev(xo(k), y, z, c)))
        fwd_y(k, i)

    def take_y(k):
        got(wp.at[0], wy_r.at[k])
        fwd_c(k, 1)

    def unpack(k, j):
        l = yl if j == 0 else 1 - yl
        q = xo(NX - k if k else 0) * 2 + l
        for cc in range(2):
            sh = q * 2 + cc
            wu[q, cc * 320:(cc + 1) * 320, 0:128] = wp[sh, 0:320, :]
            b = wp[sh, 320:480, :]
            wu[q, cc * 320:cc * 320 + 160, 128:256] = b
            wu[q, cc * 320 + 160:(cc + 1) * 320, 128:256] = pltpu.roll(
                b.astype(F32), 64, 1).astype(BF16)
        return q

    def add_logits(k, j):
        wc[(k, j)].wait_recv()
        q = unpack(k, j)
        part = jnp.dot(s[:, pl.ds(pl.multiple_of(q * QW, 128), QW)], wu[q],
                       preferred_element_type=F32)
        if (k, j) == (0, 0):
            logit[...] = part
        else:
            logit[...] += part

    for i in range(5):
        block(i)
    for i in range(4):
        take_x(1, i)
        take_x(3, (i + 2) % 4)
        if i < 3:
            block(5 + i)
    fwd_c(1, 0)
    fwd_c(3, 0)
    take_y(0)
    add_logits(0, 0)
    take_x(2, 0)
    take_x(2, 2)
    add_logits(1, 0)
    take_x(2, 1)
    take_x(2, 3)
    fwd_c(2, 0)
    add_logits(3, 0)
    add_logits(0, 1)
    add_logits(2, 0)
    take_y(1)
    take_y(3)
    add_logits(1, 1)
    take_y(2)
    add_logits(3, 1)
    add_logits(2, 1)

    lane = lax.broadcasted_iota(jnp.int32, (TOK, 256), 1)
    tcopy.wait()
    t_col = jnp.transpose(jnp.broadcast_to(tgt[...].reshape(1, TOK).astype(F32), (128, TOK)))
    tc = jnp.concatenate([t_col, t_col], axis=1)
    onehot = (tc == lane.astype(F32)).astype(F32)
    lg = jnp.where(lane < V, logit[...], -3e38)
    m = jnp.max(lg, axis=1, keepdims=True)
    e = jnp.where(lane < V, jnp.exp(lg - m), 0.0)
    p = e / jnp.sum(e, axis=1, keepdims=True)
    dl = ((p - onehot) * SCALE).astype(BF16)
    up = dl[:, 128:256].astype(F32)
    dle[:, 0:128] = dl[:, 0:128]
    dle[:, 128:256] = (up + pltpu.roll(up, 64, 1)).astype(BF16)

    lane_lo = lax.broadcasted_iota(jnp.int32, (320, 128), 1) < 64
    pick_row = lax.broadcasted_iota(jnp.int32, (8, 128), 0)
    pick_half = (lax.broadcasted_iota(jnp.int32, (8, 128), 1) >= 64).astype(jnp.int32)
    ones = jnp.ones((8, 128), BF16)
    halves = (pick_row == pick_half).astype(BF16)
    part_dev = dev(x, y, z, oc)
    g_loc[...] = jnp.zeros((16, 320), F32)

    def packed(n):
        return jnp.where(lane_lo, terms[n, 0:320, 128:256], terms[n, 320:640, 128:256])

    def x_go(l, n):
        rs = axr_r.at[l, n // 3] if n % 3 == 0 else ax_r.at[l]
        go(rcopy(ax_send.at[l, n], ax_recv.at[l, n], ax_s, rs, dev(xo(1 if n < 3 else 3), y, z, c)))

    def x_relay(l):
        for i in range(2):
            got(ax_recv.at[l, 3 * i], axr_r.at[l, i])
            ax_send[l, 3 * i + 2] = (a_pend[l, i] + ax_recv[l, 3 * i].astype(F32)).astype(BF16)
            x_go(l, 3 * i + 2)

    def row_sums(pick, v):
        hi = v.astype(BF16)
        lo = (v - hi.astype(F32)).astype(BF16)
        dims = (((1,), (1,)), ((), ()))
        return (lax.dot_general(pick, hi, dims, preferred_element_type=F32)
                + lax.dot_general(pick, lo, dims, preferred_element_type=F32))

    def by_z(src, dst):
        for j in range(NZ):
            for i in range(4):
                dst[j, 10 * i:10 * i + 16] = src[80 * i + 10 * j:80 * i + 10 * j + 16]

    def gain_a(n):
        l, k = todo[n]
        q = xo(k) * 2 + l
        wa = wu[q, pl.ds(pl.multiple_of(c * 320, 16), 320), 0:128].astype(F32)
        row = c * 8 + q
        g_loc[pl.ds(row, 1), :] += row_sums(ones, a_tot[n] * wa)[0:1]

    def gain_b(l, b):
        q = (c * 2 + b) * 2 + l
        wb = jnp.concatenate(
            [jnp.where(lane_lo[0:160], wu[q, 0:160, 128:256], wu[q, 480:640, 128:256]),
             jnp.where(lane_lo[0:160], wu[q, 160:320, 128:256], wu[q, 320:480, 128:256])],
            axis=0).astype(F32)
        t = row_sums(halves, b_tot[l * 4 + place(b), 0:320] * wb)
        g_loc[pl.ds(q, 1), :] += t[0:1]
        g_loc[pl.ds(8 + q, 1), :] += t[1:2]

    todo = [(l, k) for l in range(2) for k in (2, 1, 3, 0)]

    def place(b):
        k = lax.rem(c * 2 + b + NX - x, NX)
        return jnp.where(k == 0, 3, jnp.where(k == 3, 2, jnp.where(k == 2, 0, 1)))

    def step(n):
        r, m = n - 1, n - 3
        if 0 <= m:
            l, k = todo[m]
            xx = xo(k)
            own = lax.div(xx, 2) == c
            b = lax.rem(xx, 2)
            got(a_core.at[0], ac_r.at[m])

            @pl.when(own)
            def _():
                got(b_core.at[0], bc_r.at[m])

        if n < 8:
            q = xo(todo[n][1]) * 2 + todo[n][0]
            terms[n] = lax.dot_general(
                s[:, pl.ds(pl.multiple_of(q * QW, 128), QW)], dle[...],
                (((0,), (0,)), ((), ())), preferred_element_type=F32)
        if 0 <= r < 8:
            a_send[r] = terms[r, pl.ds(pl.multiple_of(oc * 320, 16), 320), 0:128].astype(BF16)
            b_send[r] = packed(r).astype(BF16)
        if 0 <= m:
            tot = (terms[m, pl.ds(pl.multiple_of(c * 320, 16), 320), 0:128]
                   + a_core[m].astype(F32))
            a_tot[m] = tot
            if k == 0:
                a_acc[l, 0:320] = tot
            if k == 1:
                ax_send[l, 1] = tot[160:320].astype(BF16)
                a_pend[l, 0] = tot[0:160]
            if k == 2:
                ax_send[l, 0] = tot[0:160].astype(BF16)
                ax_send[l, 3] = tot[160:320].astype(BF16)
            if k == 3:
                ax_send[l, 4] = tot[0:160].astype(BF16)
                a_pend[l, 1] = tot[160:320]
            tot = packed(m) + b_core[m].astype(F32)
            b_tot[m, 0:320] = tot
            b0_send[m] = tot.astype(BF16)
        if 0 <= r < 8:
            go(rcopy(a_send.at[r], a_core.at[r], ac_s, ac_r.at[r], part_dev))

            @pl.when(lax.div(xo(todo[r][1]), 2) != c)
            def _():
                go(rcopy(b_send.at[r], b_core.at[r], bc_s, bc_r.at[r], part_dev))

        if 0 <= m:
            for i in {0: (), 1: (1,), 2: (0, 3), 3: (4,)}[k]:
                x_go(l, i)

            @pl.when(jnp.logical_and(own, b == 0))
            def _():
                for i in range(4):
                    j = lax.rem(i * 2 + l + 8 - y, 8)

                    @pl.when(j != 0)
                    def _():
                        go(rcopy(b0_send.at[m, pl.ds(80 * i, 80)], b0_recv.at[j], b0_s, b0_r,
                                 dev(x, i * 2 + l, z, c)))

            @pl.when(jnp.logical_and(own, b == 1))
            def _():
                by_z(b_tot.at[m], b1_p32.at[l])
                b1_p16[l] = b1_p32[l].astype(BF16)
                for j in range(1, NZ):
                    go(rcopy(b1_p16.at[l, zo(j)], b1_recv.at[j, l], b1_s, b1_r, dev(x, y, zo(j), c)))

    a_acc[:, 320:336] = jnp.zeros((2, 16, 128), F32)
    b_tot[:, 320:336] = jnp.zeros((8, 16, 128), F32)
    a1_p32[:, 40:48] = jnp.zeros((8, 8, 128), F32)
    b1_p32[:, :, 40:48] = jnp.zeros((2, 8, 8, 128), F32)
    bx_own[:, 80:96] = jnp.zeros((2, 16, 128), F32)
    a_fin0[80:96] = jnp.zeros((16, 128), F32)
    b_fin[96:112] = jnp.zeros((16, 128), F32)

    for n in range(11):
        step(n)
        if n >= 8:
            gain_a(n - 8)
    x_relay(0)
    for n in range(3, 8):
        gain_a(n)
        if n == 5:
            x_relay(1)
    for l in range(2):
        for b in range(2):
            gain_b(l, b)

    grow = pl.multiple_of(c * 8, 8)
    gorow = pl.multiple_of(oc * 8, 8)
    go(rcopy(g_loc.at[pl.ds(gorow, 8)], g_core, gc_s, gc_r, part_dev))

    def spread(buf, own, ss, rs, count, to):
        for k in range(1, count):
            go(rcopy(buf.at[own], buf.at[own], ss, rs, to(k)))

    def sum8(v):
        return ((v[0] + v[1]) + (v[2] + v[3])) + ((v[4] + v[5]) + (v[6] + v[7]))

    got(g_core, gc_r)
    g_z[z] = g_loc[pl.ds(grow, 8)] + g_core[...]
    spread(g_z, z, gz_s, gz_r, NZ, lambda k: dev(x, y, zo(k), c))

    def x_done(l):
        got(ax_recv.at[l, pl.ds(0, 4)], ax_r.at[l])
        for i, (m, n) in enumerate(((4, 2), (1, 5))):
            a_acc[l, 160 * i:160 * i + 160] += ax_recv[l, m].astype(F32) + ax_recv[l, n].astype(F32)

    x_done(0)
    ay_send[...] = a_acc[0, 0:320].astype(BF16)
    for i in range(4):
        j = lax.rem(i * 2 + 8 - y, 8)

        @pl.when(j != 0)
        def _():
            go(rcopy(ay_send.at[pl.ds(80 * i, 80)], ay_recv.at[j], ay_s, ay_r, dev(x, i * 2, z, c)))

    x_done(1)
    by_z(a_acc.at[1], a1_p32)
    a1_p16[...] = a1_p32[...].astype(BF16)
    for j in range(1, NZ):
        go(rcopy(a1_p16.at[zo(j)], a1_recv.at[j], a1_s, a1_r, dev(x, y, zo(j), c)))

    got(b0_recv.at[pl.ds(1, 7)], b0_r)
    t = b_tot[yl * 4 + place(0), pl.ds(pl.multiple_of(yh * 80, 16), 80)]
    for j in range(1, NY):
        t = t + b0_recv[j].astype(F32)
    bx_own[0, 0:80] = t
    got(b1_recv.at[pl.ds(1, 7)], b1_r)
    for l in range(2):
        t = b1_p32[l, z]
        for j in range(1, NZ):
            t = t + b1_recv[j, l].astype(F32)
        bx_own[1, 48 * l:48 * l + 48] = t
    bx_send[...] = bx_own[...].astype(BF16)
    for k in range(1, NX):
        xx = xo(k)

        @pl.when(lax.div(xx, 2) == c)
        def _():
            go(rcopy(bx_send.at[lax.rem(xx, 2)], bx_recv.at[k - 1], bx_s, bx_r, dev(xx, y, z, c)))

    got(g_z.at[pl.ds(0, 7)], gz_r)
    g_y[y] = sum8(g_z)
    spread(g_y, y, gy_s, gy_r, NY, lambda k: dev(x, yo(k), z, c))

    @pl.when(yl == 0)
    def _():
        got(ay_recv.at[pl.ds(1, 7)], ay_r)
        t = a_acc[0, pl.ds(pl.multiple_of(yh * 80, 16), 80)]
        for j in range(1, NY):
            t = t + ay_recv[j].astype(F32)
        a_fin0[0:80] = t
        for i in range(NZ):
            az0_send[i] = a_fin0[10 * i:10 * i + 16]
        az_recv[z] = az0_send[z]
        for k in range(1, NZ):
            go(rcopy(az0_send.at[zo(k)], az_recv.at[z], az_s, az_r, dev(x, y, zo(k), c)))

    got(a1_recv.at[pl.ds(1, 7)], a1_r)
    t = a1_p32[z]
    for j in range(1, NZ):
        t = t + a1_recv[j].astype(F32)
    a_fin1[...] = t
    for i in range(4):
        az1_send[i] = a_fin1[10 * i:10 * i + 16]
    for i in range(4):
        @pl.when(y != 2 * i + 1)
        def _():
            go(rcopy(az1_send.at[i], az_recv.at[y], az_s, az_r, dev(x, 2 * i + 1, z, c)))

        @pl.when(y == 2 * i + 1)
        def _():
            az_recv[y] = az1_send[i]

    slot = jnp.where(odd == 1, y, z)

    @pl.when(mine)
    def _():
        got(bx_recv, bx_r)
        v = bx_recv[...].astype(F32)
        b_fin[0:96] = (bx_own[odd] + v[0]) + (v[1] + v[2])

        @pl.when(odd == 0)
        def _():
            for n in range(8):
                bz_send[n] = b_fin[10 * n:10 * n + 16].astype(BF16)

        @pl.when(odd == 1)
        def _():
            for n in range(8):
                o = (n % 2) * 48 + (n // 2) * 10
                bz_send[n] = b_fin[o:o + 16].astype(BF16)

        bz_recv[slot] = bz_send[slot]
        for k in range(8):
            n = lax.rem(slot + k, 8)
            to_y = jnp.where(odd == 1, n, y)
            to_z = jnp.where(odd == 1, z, n)
            for o in range(0 if k else 1, 2):
                go(rcopy(bz_send.at[n], bz_recv.at[slot], bz_s, bz_r, dev(x, to_y, to_z, oc if o else c)))

    got(g_y.at[pl.ds(0, 7)], gy_r)
    g_x[c, x] = sum8(g_y)
    mine_x = g_x.at[c, x]
    for k in range(1, NX):
        go(rcopy(mine_x, mine_x, gx_s, gx_r, dev(xo(k), y, z, c)))
    for k in range(NX):
        go(rcopy(mine_x, mine_x, gx_s, gx_r, dev(xo(k), y, z, oc)))

    got(az_recv.at[pl.ds(0, 7)], az_r)
    wg_out[:, 0:128] = sum8(az_recv)[0:10]

    @pl.when(mine)
    def _():
        got(bz_recv.at[pl.ds(0, 7)], bz_r)

    @pl.when(jnp.logical_not(mine))
    def _():
        got(bz_recv, bz_r)

    tb = sum8(bz_recv[...].astype(F32))
    tb = jnp.where(c == 0, tb, pltpu.roll(tb, 64, 1))
    wg_out[:, 128:192] = tb[0:10, 0:64]

    got(g_z.at[pl.ds(0, 7)], gx_r)
    for i in range(2):
        gg_out[8 * i:8 * i + 8] = (g_x[i, 0] + g_x[i, 1]) + (g_x[i, 2] + g_x[i, 3])

    sent(wp.at[pl.ds(0, 3)], wx_s)
    sent(wp.at[pl.ds(0, 4)], wy_s)
    sent(wp.at[pl.ds(0, 8)], wc_s)
    sent(a_send, ac_s)
    sent(b_send.at[pl.ds(0, 4)], bc_s)
    sent(ax_send, ax_s)
    sent(g_core, gc_s)
    sent(g_z.at[pl.ds(0, 7)], gz_s)
    sent(g_y.at[pl.ds(0, 7)], gy_s)
    sent(g_z.at[pl.ds(0, 7)], gx_s)
    sent(b0_recv.at[pl.ds(1, 7)], b0_s)
    sent(b1_recv.at[pl.ds(1, 7)], b1_s)
    sent(a1_recv.at[pl.ds(1, 7)], a1_s)

    @pl.when(yl == 0)
    def _():
        sent(ay_recv.at[pl.ds(0, 3)], ay_s)
        sent(az_recv.at[pl.ds(0, 7)], az_s)
        sent(az_recv.at[pl.ds(0, 4)], az_s)

    @pl.when(yl == 1)
    def _():
        sent(ay_recv.at[pl.ds(0, 4)], ay_s)
        sent(az_recv.at[pl.ds(0, 3)], az_s)

    @pl.when(mine)
    def _():
        sent(bx_recv.at[0], bx_s)
        sent(bz_recv, bz_s)
        sent(bz_recv.at[pl.ds(0, 7)], bz_s)

    @pl.when(jnp.logical_not(mine))
    def _():
        sent(bx_recv.at[pl.ds(0, 2)], bx_s)


def leave(wg_in, gg_in, gain, wg_out, gg_out):
    wg_out[...] = wg_in[...]
    both = jnp.concatenate([gg_in[0:8], gg_in[8:16]], axis=1)
    for q in range(8):
        for i in range(5):
            r = q * 5 + i
            gg_out[r:r + 1] = both[q:q + 1, 128 * i:128 * i + 128] / gain[r:r + 1]


def on_device(hidden, targets, head_weight, norm_gain):
    dma = pltpu.SemaphoreType.DMA
    vm = pltpu.VMEM
    scratch = [
        vm((TOK,), jnp.int32), vm((192, 320), BF16), vm((1, D), F32),
        vm((TOK, D), BF16), vm((TOK, D), BF16),
        vm((16, 480, 128), BF16), vm((8, QW, 256), BF16), vm((TOK, 256), F32), vm((TOK, 256), BF16),
        vm((8, QW, 256), F32), vm((8, 320, 128), BF16), vm((8, 320, 128), BF16),
        vm((8, 320, 128), F32), vm((8, 320, 128), BF16), vm((8, 320, 128), BF16),
        vm((8, 336, 128), F32),
        vm((2, 6, 160, 128), BF16), vm((2, 6, 160, 128), BF16), vm((2, 2, 160, 128), F32),
        vm((2, 336, 128), F32),
        vm((320, 128), BF16), vm((8, 80, 128), BF16),
        vm((8, 48, 128), F32), vm((8, 48, 128), BF16), vm((8, 48, 128), BF16),
        vm((96, 128), F32), vm((48, 128), F32),
        vm((8, 16, 128), F32), vm((4, 16, 128), F32), vm((8, 16, 128), F32),
        vm((8, 320, 128), BF16), vm((8, 80, 128), BF16),
        vm((2, 8, 48, 128), F32), vm((2, 8, 48, 128), BF16), vm((8, 2, 48, 128), BF16),
        vm((2, 96, 128), F32), vm((2, 96, 128), BF16), vm((3, 96, 128), BF16),
        vm((112, 128), F32), vm((8, 16, 128), BF16), vm((8, 16, 128), BF16),
        vm((16, 320), F32), vm((8, 320), F32), vm((2, 4, 8, 320), F32),
        vm((8, 8, 320), F32), vm((8, 8, 320), F32),
        dma((7,)),
        dma, dma((3, 4)), dma, dma((4,)), dma, dma((4, 2)), dma, dma((8,)), dma, dma((8,)),
        dma, dma((2, 2)), dma((2,)), dma, dma, dma, dma, dma, dma,
        dma, dma, dma, dma, dma, dma, dma, dma,
        dma, dma, dma, dma, dma, dma, dma, dma,
    ]
    vspec = pl.BlockSpec(memory_space=pltpu.VMEM)
    wg, gg = pl.pallas_call(
        kernel,
        out_shape=(jax.ShapeDtypeStruct((10, V), F32), jax.ShapeDtypeStruct((16, 320), F32)),
        in_specs=[pl.BlockSpec(memory_space=pl.ANY)] * 4,
        out_specs=(vspec, vspec),
        scratch_shapes=scratch,
        compiler_params=pltpu.CompilerParams(
            collective_id=0, has_side_effects=True, vmem_limit_bytes=56 * 1024 * 1024),
        cost_estimate=pl.CostEstimate(flops=3 * 2 * TOK * D * V, bytes_accessed=TOK * D * 2,
                                      transcendentals=TOK * V),
    )(hidden, targets, head_weight.T, norm_gain.reshape(1, D))
    wg, gg = pl.pallas_call(
        leave,
        out_shape=(jax.ShapeDtypeStruct((10, V), F32), jax.ShapeDtypeStruct((40, 128), F32)),
        in_specs=[vspec] * 3,
        out_specs=(vspec, vspec),
    )(wg, gg, norm_gain.reshape(40, 128))
    return wg, gg.reshape(D)


def solution(mesh):
    placed = (P(("section", "dp"), None), P(("section", "dp")), P("section", None), P())
    return jax.shard_map(
        on_device,
        mesh=mesh,
        in_specs=placed,
        out_specs=(P(("section", "dp"), None), P()),
        check_vma=False,
    )
```
